256 devices in a mesh: traj: 8 (over y, core), feat: 32 (over x, z).
Axes of the slice: x: 4, y: 4, z: 8, core: 2. Of those that a mesh axis runs over, the one named last changes fastest.
Arguments:
- frame_values: bfloat16 [40960, 8, 128], P(('traj', 'feat')), may hold values from 0 to 2
- frame_blocks: int32 [40960, 8], P(('traj', 'feat')), may hold values from 0 to 31, all different within a row
- lag_pairs: int32 [32768, 2], P(('traj', 'feat')), may hold values from 0 to 159, as said below
Outputs:
- cov_inst: float32 [4096, 4096], P('traj', 'feat')
- cov_lag: float32 [4096, 4096], P('traj', 'feat')
The draws below stay inside these ranges and needn't reach their ends.
Inputs may be any that keep to these rules, and one draw needn't show every extreme that they name: `frame_blocks`: the 8 blocks of one frame are different. `lag_pairs`: on each device the first entries take every value of 0 to 127 once; the second entry lies 1 to 32 frames after the first.
All inputs are finite; a program needn't handle non-finite values.
Results may differ from the reference program's by a relative error of at most 0.0003.
Values may be sent and summed in bfloat16 or wider, within the bound.
A program may use at most 256 MiB of HBM per device.

```python
import math
import jax
import jax.numpy as jnp
from jax import lax

NF = 4096
BLOCK = 128
NBLK = 32
ACTIVE = 8
TAU = 32
PAIRS_DEV = 128
FR_DEV = 160
FRAMES = 40960
PAIRS = 32768


def draw_lag_pairs(key, part):
    key = jax.random.fold_in(key, 7)
    shard_count = PAIRS // PAIRS_DEV
    order_key, lag_key = jax.random.split(key)
    starts = jax.vmap(lambda one_key: jax.random.permutation(one_key, PAIRS_DEV))(jax.random.split(order_key, shard_count)).astype(jnp.int32)
    spacing = jax.random.randint(lag_key, (shard_count, PAIRS_DEV), 1, TAU + 1).astype(jnp.int32)
    spacing = jnp.where(starts == PAIRS_DEV - 1, TAU, spacing).astype(jnp.int32)
    return jnp.stack([starts, starts + spacing], axis=-1).reshape(PAIRS, 2).astype(jnp.int32)


def block_scale(key, dims, pieces, smallest, largest):
    loudness, own = 1.0, jax.random.fold_in(key, 6)
    for axis_at, parts in pieces:
        steps = jnp.exp(jax.random.uniform(jax.random.fold_in(own, axis_at), (parts,), jnp.float32, smallest / len(pieces), largest / len(pieces)))
        loudness = loudness * jnp.repeat(steps, dims[axis_at] // parts).reshape([-1 if axis == axis_at else 1 for axis in range(len(dims))])
    return loudness


def different_ones(rng, rows, number_of, top, lift):
    ranking = jax.random.permutation(jax.random.fold_in(rng, 1), number_of)
    favour = ranking
    for power in range(3):
        favour = favour * favour // number_of
    favour = favour * lift // number_of
    tickets = jax.random.randint(jax.random.fold_in(rng, 2), (rows, number_of), 0, 4096) + favour
    fixed_rows = jax.random.permutation(jax.random.fold_in(rng, 3), rows)[jnp.arange(number_of) % rows]
    tickets = jnp.where(jnp.arange(rows)[:, None] == fixed_rows[None, :], 1 << 14, tickets)
    priority = tickets * number_of + jnp.arange(number_of)
    return lax.top_k(priority.astype(jnp.int32), top)[1].astype(jnp.int32)


def setup_inputs(seed: int = 0) -> dict:
    key_of = jax.random.split(jax.random.key(seed), 4)
    frame_values = jnp.clip(2.0 * jax.random.uniform(key_of[0], (FRAMES, ACTIVE, BLOCK), jnp.float32) ** block_scale(key_of[0], (FRAMES, ACTIVE, BLOCK), ((0, 256),), -0.2, 0.2), 0.0, 2.0).astype(jnp.bfloat16)
    frame_blocks = different_ones(key_of[1], FRAMES, NBLK, ACTIVE, 2048)
    lag_pairs = draw_lag_pairs(jax.random.fold_in(key_of[3], 71), 0)
    return dict(frame_values=frame_values, frame_blocks=frame_blocks, lag_pairs=lag_pairs)


def spread(values, blocks):
    count_blocks = NF // BLOCK
    onehot = (blocks[:, :, None] == jnp.arange(count_blocks, dtype=jnp.int32)[None, None, :]).astype(jnp.float32)
    filled = jnp.einsum("rkn,rkb->rnb", onehot, values.astype(jnp.float32))
    return filled.reshape(values.shape[0], NF)


def reference(frame_values, frame_blocks, lag_pairs):
    shard_count = PAIRS // PAIRS_DEV
    group_size = math.gcd(shard_count, 8)
    steps_count = shard_count // group_size
    values = frame_values.reshape(steps_count, group_size, FR_DEV, ACTIVE, BLOCK)
    blocks = frame_blocks.reshape(steps_count, group_size, FR_DEV, ACTIVE)
    pair_rows = lag_pairs.reshape(steps_count, group_size, PAIRS_DEV, 2)
    select_rows = jax.vmap(lambda source_table, row_index: source_table[row_index])

    def advance(running, scan_item):
        shard_values, shard_blocks, shard_pairs = scan_item
        first_index = shard_pairs[:, :, 0]
        second_index = shard_pairs[:, :, 1]
        start_rows = spread(select_rows(shard_values, first_index).reshape(-1, ACTIVE, BLOCK),
                            select_rows(shard_blocks, first_index).reshape(-1, ACTIVE))
        lagged_rows = spread(select_rows(shard_values, second_index).reshape(-1, ACTIVE, BLOCK),
                             select_rows(shard_blocks, second_index).reshape(-1, ACTIVE))
        plain_sums = running[0] + jnp.dot(start_rows.T, start_rows, precision=lax.Precision.HIGHEST)
        lagged_sums = running[1] + jnp.dot(start_rows.T, lagged_rows, precision=lax.Precision.HIGHEST)
        start_sum = running[2] + jnp.sum(start_rows, axis=0)
        lagged_sum = running[3] + jnp.sum(lagged_rows, axis=0)
        return (plain_sums, lagged_sums, start_sum, lagged_sum), None

    start_state = (jnp.zeros((NF, NF), jnp.float32), jnp.zeros((NF, NF), jnp.float32),
                   jnp.zeros((NF,), jnp.float32), jnp.zeros((NF,), jnp.float32))
    final_state, unused = lax.scan(advance, start_state, (values, blocks, pair_rows))
    plain_sums, lagged_sums, start_sum, lagged_sum = final_state
    mean_start = start_sum / PAIRS
    mean_lagged = lagged_sum / PAIRS
    cov_inst = plain_sums / PAIRS - jnp.outer(mean_start, mean_start)
    cov_lag = lagged_sums / PAIRS - jnp.outer(mean_start, mean_lagged)
    return cov_inst, cov_lag
```

```python
import functools

import jax
import jax.numpy as jnp
from jax import lax
from jax.experimental import pallas as pl
from jax.experimental.pallas import tpu as pltpu
from jax.sharding import PartitionSpec as P

MESH = pl.DeviceIdType.MESH
F32, BF16 = jnp.float32, jnp.bfloat16
NX, NY, NZ = 4, 4, 8
B = 128
SLOTS = 8
FRAMES = 160
EXTRA = FRAMES - B
IDS = 10 * B
PACKET = IDS + 16
HALF = 5 * B
CHUNK = 4 * B + 8
CUT = 264
PAIRS = 32768
NT = (((1,), (1,)), ((), ()))


def place():
    t, f = lax.axis_index("traj"), lax.axis_index("feat")
    return f // NZ, t // 2, f % NZ, t % 2


def prepare(values, blocks, pairs, packet, plain, index):
    plain[...] = values[...].astype(F32).reshape(FRAMES * SLOTS, B)
    for k in range(SLOTS):
        tile = plain[pl.ds(k, B, stride=SLOTS), :]
        packet[k * B : (k + 1) * B, :] = tile.T.astype(BF16)
    for g in range(2):
        tile = jnp.concatenate(
            [plain[pl.ds(B * SLOTS + 4 * g + i, EXTRA, stride=SLOTS), :] for i in range(4)], axis=0
        )
        packet[(SLOTS + g) * B : (SLOTS + g + 1) * B, :] = tile.T.astype(BF16)
    index[...] = jnp.zeros_like(index)
    index[:, 0:SLOTS] = blocks[...].astype(F32)
    first = index[0:B, :].T[0:SLOTS, :]
    rest = jnp.concatenate([index[B:FRAMES, :]] * 4, axis=0).T
    lane = lax.broadcasted_iota(jnp.int32, (1, B), 1) // EXTRA
    rows = [first]
    for g in range(2):
        row = jnp.zeros((1, B), F32)
        for i in range(4):
            row = jnp.where(lane == i, rest[4 * g + i : 4 * g + i + 1, :], row)
        rows.append(row)
    start, lagged = pairs[:, 0:1], pairs[:, 1:2]
    here = start == lax.broadcasted_iota(jnp.int32, (B, B), 1)
    rows.append(jnp.sum(jnp.where(here, lagged.astype(F32), 0.0), axis=0, keepdims=True))
    rows.append(jnp.zeros((5, B), F32))
    packet[IDS:PACKET, :] = jnp.concatenate(rows, axis=0).astype(BF16)


def fill(source, lanes, core, z, dense_rows, dense_cols, picked, picks):
    ids = source[IDS:PACKET, :].astype(F32)
    wide = [jnp.broadcast_to(ids[k : k + 1, :], (16, B)).astype(BF16) for k in range(SLOTS + 2)]
    none = jnp.zeros((16, B), BF16)

    def block(number, put):
        want = jnp.full((16, B), number, jnp.int32).astype(F32).astype(BF16)
        masks = [w == want for w in wide[:SLOTS]]
        for j in range(0, B, 16):
            got = none
            for k in range(SLOTS):
                got = jnp.where(masks[k], source[k * B + j : k * B + j + 16, :], got)
            put(j, got)
        return want

    def rows_of(n, carry):
        def put(j, got):
            dense_rows[pl.ds(pl.multiple_of(n * B + j, 16), 16), lanes] = got

        block(n // 4 * NZ + core * 4 + n % 4, put)
        return carry

    lax.fori_loop(0, 4 * NY, rows_of, 0)

    def cols_of(n, carry):
        def put(j, got):
            dense_cols[n, j : j + 16, lanes] = got
            picked[pl.ds(pl.multiple_of(n * B + j, 16), 16), 0:B] = got

        want = block(n * NZ + z, put)
        for g in range(2):
            mask = wide[SLOTS + g] == want
            for j in range(0, B, 16):
                tile = source[(SLOTS + g) * B + j : (SLOTS + g) * B + j + 16, :]
                picked[pl.ds(pl.multiple_of(n * B + j, 16), 16), (g + 1) * B : (g + 2) * B] = (
                    jnp.where(mask, tile, none)
                )
        return carry

    lax.fori_loop(0, NX, cols_of, 0)
    down = lax.broadcasted_iota(jnp.int32, (B, B), 0).astype(F32)
    rest = (lax.broadcasted_iota(jnp.int32, (B, B), 0) % EXTRA + B).astype(F32)
    lag = jnp.broadcast_to(ids[SLOTS + 2 : SLOTS + 3, :], (B, B))
    picks[0:B, :] = jnp.where(lag == down, 1.0, 0.0).astype(BF16)
    tail = jnp.where(lag == rest, 1.0, 0.0).astype(BF16)
    picks[B : 2 * B, :] = tail
    picks[2 * B : 3 * B, :] = tail

    def lags_of(n, carry):
        part = picked[pl.ds(pl.multiple_of(n * B, B), B), :]
        dense_cols[n, B : 2 * B, lanes] = jnp.dot(
            part, picks[...], preferred_element_type=F32
        ).astype(BF16)
        return carry

    lax.fori_loop(0, NX, lags_of, 0)


def multiply(first, depth, dense_rows, dense_cols, inst, lag, row_sums, col_sums):
    def tile(n, carry):
        x, y = n // NY, n % NY
        rows = pl.ds(pl.multiple_of(y * 4 * B, 4 * B), 4 * B)
        out = lax.dot_general(
            dense_rows[rows, 0:depth], dense_cols[x, :, 0:depth], NT, preferred_element_type=F32
        )
        if first:
            inst[x, y, 0 : 4 * B, :] = out[:, 0:B]
            lag[y, x, 0 : 4 * B, :] = out[:, B : 2 * B]
        else:
            inst[x, y, 0 : 4 * B, :] += out[:, 0:B]
            lag[y, x, 0 : 4 * B, :] += out[:, B : 2 * B]
        return carry

    lax.fori_loop(0, NX * NY, tile, 0)

    def row_tile(y, carry):
        rows = pl.ds(pl.multiple_of(y * 4 * B, 4 * B), 4 * B)
        out = lax.dot_general(
            dense_rows[rows, 0:depth], jnp.ones((B, depth), BF16), NT, preferred_element_type=F32
        )
        if first:
            row_sums[rows, :] = out
        else:
            row_sums[rows, :] += out
        return carry

    lax.fori_loop(0, NY, row_tile, 0)

    def col_tile(x, carry):
        out = lax.dot_general(
            jnp.ones((8, depth), BF16), dense_cols[x, :, 0:depth], NT, preferred_element_type=F32
        )
        if first:
            col_sums[x] = out
        else:
            col_sums[x] += out
        return carry

    lax.fori_loop(0, NX, col_tile, 0)


def sums_into(row_sums, col_sums, inst, lag):
    diagonal = lax.broadcasted_iota(jnp.int32, (B, B), 0) == lax.broadcasted_iota(
        jnp.int32, (B, B), 1
    )

    def of_rows(y, carry):
        flat = []
        for i in range(4):
            tile = row_sums[pl.ds(pl.multiple_of(y * 4 * B + i * B, B), B), :]
            flat.append(jnp.sum(jnp.where(diagonal, tile, 0.0), axis=0, keepdims=True))

        def of_cols(x, inner):
            sums = col_sums[x]
            inst[x, y, 4 * B : CHUNK, :] = jnp.concatenate(flat + [sums[0:4, 0:B]], axis=0)
            lag[y, x, 4 * B : CHUNK, :] = jnp.concatenate(flat + [sums[0:4, B : 2 * B]], axis=0)
            return inner

        return lax.fori_loop(0, NX, of_cols, carry)

    lax.fori_loop(0, NY, of_rows, 0)


def add_rows(target, addends, start, count):
    step = 8 if count % 64 else 64

    def body(n, carry):
        rows = pl.ds(pl.multiple_of(start + n * step, 8), step)
        total = target[rows, :]
        for a in addends:
            total = total + a[rows, :]
        target[rows, :] = total
        return carry

    lax.fori_loop(0, count // step, body, 0)


def kernel(
    values, blocks, pairs, inst_out, lag_out,
    plain, index, ring, pair, dense_rows, dense_cols, picked, picks,
    inst, lag, row_sums, col_sums, far1, near1, far2, near2,
    ring_send, ring_recv, pair_send, pair_recv, rs_send, rs_recv,
):
    x, y, z, core = place()

    def device(dx=0, dy=0, dz=0, dc=0):
        return (
            lax.rem(y + dy + NY, NY) * 2 + lax.rem(core + dc, 2),
            lax.rem(x + dx + NX, NX) * NZ + lax.rem(z + dz + NZ, NZ),
        )

    def send(source, target, send_sem, recv_sem, to):
        copy = pltpu.make_async_remote_copy(
            src_ref=source, dst_ref=target, send_sem=send_sem, recv_sem=recv_sem,
            device_id=to, device_id_type=MESH,
        )
        copy.start()
        return copy

    up, down, other = device(dz=1), device(dz=-1), device(dc=1)
    barrier = pltpu.get_barrier_semaphore()
    for to in (up, down, other, device(dx=1), device(dx=-1), device(dy=1), device(dy=-1)):
        pl.semaphore_signal(barrier, inc=1, device_id=to, device_id_type=MESH)

    prepare(values, blocks, pairs, ring.at[0], plain, index)
    pl.semaphore_wait(barrier, 7)

    started = []

    def share(slot, rows, sem):
        started.append(
            send(ring.at[slot, rows], pair.at[slot, rows], pair_send.at[sem], pair_recv.at[sem], other)
        )
        return started[-1]

    whole = pl.ds(0, PACKET)
    low, high = pl.ds(0, HALF), pl.ds(HALF, PACKET - HALF)
    right = send(ring.at[0], ring.at[1], ring_send.at[1], ring_recv.at[1], up)
    left = send(ring.at[0], ring.at[4], ring_send.at[4], ring_recv.at[4], down)
    shared = share(0, whole, 0)

    def fill_from(buffer, slot, position):
        lanes = pl.ds(position * B, B)
        fill(buffer.at[slot], lanes, core, z, dense_rows, dense_cols, picked, picks)

    def product(first, depth):
        multiply(first, depth, dense_rows, dense_cols, inst, lag, row_sums, col_sums)

    fill_from(ring, 0, 0)
    shared.wait_recv()
    fill_from(pair, 0, 1)
    product(True, 2 * B)

    for s in range(1, 4):
        right.wait_recv()
        started.append(right)
        if s < 3:
            right = send(ring.at[s], ring.at[s + 1], ring_send.at[s + 1], ring_recv.at[s + 1], up)
        else:
            right = send(ring.at[s, low], ring.at[7, low], ring_send.at[7], ring_recv.at[7], up)
        left.wait_recv()
        started.append(left)
        if s < 3:
            left = send(ring.at[3 + s], ring.at[4 + s], ring_send.at[4 + s], ring_recv.at[4 + s], down)
        else:
            left = send(ring.at[6, high], ring.at[7, high], ring_send.at[8], ring_recv.at[8], down)
        shared = [share(s, whole, s), share(3 + s, whole, 3 + s)]

        def from_ring(n, carry, s=s):
            fill_from(ring, s + 3 * n, n)
            return carry

        lax.fori_loop(0, 2, from_ring, 0)
        for copy in shared:
            copy.wait_recv()

        def from_pair(n, carry, s=s):
            fill_from(pair, s + 3 * n, 2 + n)
            return carry

        lax.fori_loop(0, 2, from_pair, 0)
        product(False, 4 * B)

    right.wait_recv()
    shared = [share(7, low, 7)]
    left.wait_recv()
    shared.append(share(7, high, 8))
    started += [right, left]
    fill_from(ring, 7, 0)
    for copy in shared:
        copy.wait_recv()
    fill_from(pair, 7, 1)
    product(False, 2 * B)
    sums_into(row_sums, col_sums, inst, lag)

    def axes(which):
        if which == 0:
            return inst, x, y, (device(dx=1), device(dx=-1)), (device(dy=1), device(dy=-1))
        return lag, y, x, (device(dy=1), device(dy=-1)), (device(dx=1), device(dx=-1))

    halves = (pl.ds(0, 2), pl.ds(2, 2))
    cuts = (pl.ds(0, CUT), pl.ds(CUT, CHUNK - CUT))

    def rs_copy(which, number, source, target, to):
        started.append(
            send(source, target, rs_send.at[which, number], rs_recv.at[which, number], to)
        )
        return started[-1]

    far, near, joint = {}, {}, {}
    for which in range(2):
        acc, a, _, to, _ = axes(which)
        for d in range(2):
            far[which, d] = rs_copy(
                which, d, acc.at[lax.rem(a + 2, 4), halves[d]], far1.at[which, d], to[d]
            )
    for which in range(2):
        acc, a, _, to, _ = axes(which)
        for d in range(2):
            near[which, d] = rs_copy(
                which, 2 + d, acc.at[lax.rem(a + 1 + 2 * d, 4), halves[1 - d]],
                near1.at[which, d, halves[1 - d]], to[d],
            )
    for d in range(2):
        for which in range(2):
            acc, a, _, to, _ = axes(which)
            far[which, d].wait_recv()
            target = lax.rem(a + 1 + 2 * d, 4)
            for h in range(2):
                add_rows(acc.at[target, 2 * d + h], [far1.at[which, d, h]], 0, CHUNK)
            joint[which, d] = rs_copy(
                which, 4 + d, acc.at[target, halves[d]], near1.at[which, d, halves[d]], to[d]
            )
    for which in range(2):
        acc, a, _, _, _ = axes(which)
        for d in range(2):
            near[which, d].wait_recv()
            joint[which, d].wait_recv()

        def summed(h, carry, which=which, acc=acc, a=a):
            add_rows(acc.at[a, h], [near1.at[which, 0, h], near1.at[which, 1, h]], 0, CHUNK)
            return carry

        lax.fori_loop(0, 4, summed, 0)
        acc, a, b, _, to = axes(which)
        for d in range(2):
            far[which, d] = rs_copy(
                which, 6 + d, acc.at[a, lax.rem(b + 2, 4), cuts[d]], far2.at[which, d, cuts[d]], to[d]
            )
        for d in range(2):
            near[which, d] = rs_copy(
                which, 8 + d, acc.at[a, lax.rem(b + 1 + 2 * d, 4), cuts[1 - d]],
                near2.at[which, d, cuts[1 - d]], to[d],
            )
    for which in range(2):
        acc, a, b, _, to = axes(which)
        for d in range(2):
            far[which, d].wait_recv()
            target = lax.rem(b + 1 + 2 * d, 4)
            add_rows(
                acc.at[a, target], [far2.at[which, d]], CUT * d, CUT if d == 0 else CHUNK - CUT
            )
            joint[which, d] = rs_copy(
                which, 10 + d, acc.at[a, target, cuts[d]], near2.at[which, d, cuts[d]], to[d]
            )
    for which, out in ((0, inst_out), (1, lag_out)):
        acc, a, b, _, _ = axes(which)
        for d in range(2):
            near[which, d].wait_recv()
            joint[which, d].wait_recv()
        out[...] = acc[a, b] + near2[which, 0] + near2[which, 1]
    for copy in started:
        copy.wait_send()


def on_device(frame_values, frame_blocks, lag_pairs):
    chunk = jax.ShapeDtypeStruct((CHUNK, B), F32)
    vmem = pl.BlockSpec(memory_space=pltpu.VMEM)
    inst, lag = pl.pallas_call(
        kernel,
        out_shape=(chunk, chunk),
        in_specs=[vmem] * 3,
        out_specs=(vmem, vmem),
        scratch_shapes=[
            pltpu.VMEM((FRAMES * SLOTS, B), F32),
            pltpu.VMEM((FRAMES, B), F32),
            pltpu.VMEM((NZ, PACKET, B), BF16),
            pltpu.VMEM((NZ, PACKET, B), BF16),
            pltpu.VMEM((4 * NY * B, 4 * B), BF16),
            pltpu.VMEM((NX, 2 * B, 4 * B), BF16),
            pltpu.VMEM((NX * B, 3 * B), BF16),
            pltpu.VMEM((3 * B, B), BF16),
            pltpu.VMEM((NX, NY, CHUNK, B), F32),
            pltpu.VMEM((NY, NX, CHUNK, B), F32),
            pltpu.VMEM((4 * NY * B, B), F32),
            pltpu.VMEM((NX, 8, 2 * B), F32),
            pltpu.VMEM((2, 2, 2, CHUNK, B), F32),
            pltpu.VMEM((2, 2, 4, CHUNK, B), F32),
            pltpu.VMEM((2, 2, CHUNK, B), F32),
            pltpu.VMEM((2, 2, CHUNK, B), F32),
            pltpu.SemaphoreType.DMA((9,)),
            pltpu.SemaphoreType.DMA((9,)),
            pltpu.SemaphoreType.DMA((9,)),
            pltpu.SemaphoreType.DMA((9,)),
            pltpu.SemaphoreType.DMA((2, 12)),
            pltpu.SemaphoreType.DMA((2, 12)),
        ],
        compiler_params=pltpu.CompilerParams(
            collective_id=0, has_side_effects=True, vmem_limit_bytes=56 << 20
        ),
        name="covariances",
    )(frame_values, frame_blocks, lag_pairs)
    rows = inst[4 * B : 4 * B + 4].reshape(4 * B, 1) / PAIRS
    cov_inst = inst[: 4 * B] / PAIRS - rows * (inst[4 * B + 4 : 4 * B + 5] / PAIRS)
    cov_lag = lag[: 4 * B] / PAIRS - rows * (lag[4 * B + 4 : 4 * B + 5] / PAIRS)
    return cov_inst, cov_lag


def solution(mesh):
    spec = P(("traj", "feat"))
    return jax.shard_map(
        on_device,
        mesh=mesh,
        in_specs=(spec, spec, spec),
        out_specs=(P("traj", "feat"), P("traj", "feat")),
        check_vma=False,
    )
```

```python
import jax
import jax.numpy as jnp
from jax import lax
from jax.experimental import pallas as pl
from jax.experimental.pallas import tpu as pltpu
from jax.sharding import PartitionSpec as P

MESH = pl.DeviceIdType.MESH
F32, BF16, I16, I32 = jnp.float32, jnp.bfloat16, jnp.int16, jnp.int32
NX, NY, NZ = 4, 4, 8
B = 128
SLOTS = 8
FRAMES = 160
EXTRA = FRAMES - B
IDS = 10 * B
PACKET = IDS + 16
HALF = 5 * B
ROWS = 4 * NY * B
COLS = 2 * NX * B
GROUP = 2 * NZ * B
PAIRS = NX * NY * GROUP
FAR = 8 * B + 16
NEAR = 2 * B + 16
STEPS = 16.0
TOP = 32512.0
NT = (((1,), (1,)), ((), ()))
TN = (((0,), (0,)), ((), ()))


def place():
    t, f = lax.axis_index("traj"), lax.axis_index("feat")
    return f // NZ, t // 2, f % NZ, t % 2


def prepare(values, blocks, pairs, packet, plain, index):
    plain[...] = values[...].astype(F32).reshape(FRAMES * SLOTS, B)
    for k in range(SLOTS):
        tile = plain[pl.ds(k, B, stride=SLOTS), :]
        packet[k * B : (k + 1) * B, :] = tile.T.astype(BF16)
    for g in range(2):
        tile = jnp.concatenate(
            [plain[pl.ds(B * SLOTS + 4 * g + i, EXTRA, stride=SLOTS), :] for i in range(4)], axis=0
        )
        packet[(SLOTS + g) * B : (SLOTS + g + 1) * B, :] = tile.T.astype(BF16)
    rows = [blocks[:, 0:B].astype(F32)]
    index[...] = jnp.zeros_like(index)
    index[:, 0:EXTRA] = blocks[:, B:FRAMES].astype(F32)
    rest = index[...]
    lane = lax.broadcasted_iota(I32, (1, B), 1) // EXTRA
    wide = rest
    for i in range(1, 4):
        wide = wide + pltpu.roll(rest, i * EXTRA, 1)
    for g in range(2):
        row = jnp.zeros((1, B), F32)
        for i in range(4):
            row = jnp.where(lane == i, wide[4 * g + i : 4 * g + i + 1, :], row)
        rows.append(row)
    start = jnp.broadcast_to(pairs[0:1, :], (B, B))
    here = jnp.where(start == lax.broadcasted_iota(I32, (B, B), 0), 1.0, 0.0).astype(BF16)
    lagged = jnp.broadcast_to(pairs[1:2, :], (16, B)).astype(F32).astype(BF16)
    rows.append(lax.dot_general(lagged, here, NT, preferred_element_type=F32)[0:1, :])
    rows.append(jnp.zeros((5, B), F32))
    packet[IDS:PACKET, :] = jnp.concatenate(rows, axis=0).astype(BF16)


def fill(source, lanes, core, z, dense_rows, dense_cols, picked, picks):
    ids = source[IDS:PACKET, :].astype(F32)
    wide = [jnp.broadcast_to(ids[k : k + 1, :], (16, B)).astype(BF16) for k in range(SLOTS + 2)]
    none = jnp.zeros((16, B), BF16)

    def block(number, put):
        want = jnp.full((16, B), number, I32).astype(F32).astype(BF16)
        masks = [w == want for w in wide[:SLOTS]]
        for j in range(0, B, 16):
            got = none
            for k in range(SLOTS):
                got = jnp.where(masks[k], source[k * B + j : k * B + j + 16, :], got)
            put(j, got)
        return want

    lag = jnp.broadcast_to(ids[SLOTS + 2 : SLOTS + 3, :], (B, B))
    down = lax.broadcasted_iota(I32, (B, B), 0)
    picks[0:B, :] = jnp.where(lag == down.astype(F32), 1.0, 0.0).astype(BF16)
    picks[B : 2 * B, :] = jnp.where(lag == (down % EXTRA + B).astype(F32), 1.0, 0.0).astype(BF16)

    def cols_of(n, carry):
        def put(j, got):
            dense_cols[pl.ds(pl.multiple_of(n * 2 * B + j, 16), 16), lanes] = got
            picked[pl.ds(pl.multiple_of(n * B + j, 16), 16), 0:B] = got

        want = block(n * NZ + z, put)
        masks = [wide[SLOTS + g] == want for g in range(2)]
        for j in range(0, B, 16):
            got = none
            for g in range(2):
                tile = source[(SLOTS + g) * B + j : (SLOTS + g) * B + j + 16, :]
                got = jnp.where(masks[g], tile, got)
            picked[pl.ds(pl.multiple_of(n * B + j, 16), 16), B : 2 * B] = got
        return carry

    lax.fori_loop(0, NX, cols_of, 0)
    lags = jnp.dot(picked[...], picks[...], preferred_element_type=F32).astype(BF16)
    for n in range(NX):
        dense_cols[(2 * n + 1) * B : (2 * n + 2) * B, lanes] = lags[n * B : (n + 1) * B, :]

    def rows_of(n, carry):
        def put(j, got):
            dense_rows[pl.ds(pl.multiple_of(n * B + j, 16), 16), lanes] = got

        block(n // 4 * NZ + core * 4 + n % 4, put)
        return carry

    lax.fori_loop(0, 4 * NY, rows_of, 0)


def multiply(first, depth, dense_rows, dense_cols, inst, lag, row_sums, col_sums):
    def put(ref, index, value):
        if first:
            ref[index] = value
        else:
            ref[index] += value

    half = ROWS // 2
    for q in range(2):
        height = half + 16 * q
        out = lax.dot_general(
            dense_rows[q * half : q * half + height, 0:depth], dense_cols[:, 0:depth], NT,
            preferred_element_type=F32,
        )
        for h in range(2):
            part = out[h * 4 * B : (h + 1) * 4 * B]
            for x in range(NX):
                put(inst, (x, 2 * q + h), part[:, 2 * x * B : (2 * x + 1) * B])
                put(lag, (2 * q + h, x), part[:, (2 * x + 1) * B : (2 * x + 2) * B])
            put(row_sums, (2 * q + h,), part[:, COLS:])
        if q == 1:
            for n in range(2 * NX):
                put(col_sums, (n,), out[half : half + 8, n * B : (n + 1) * B])


def encode(value):
    top = jnp.max(jnp.abs(value), axis=0, keepdims=True)
    power = jnp.ceil(jnp.log(jnp.maximum(top, 1e-30)) * (STEPS / 0.6931471805599453))
    whole = jnp.floor(value * (jnp.exp2(power * (-1 / STEPS)) * TOP) + 0.5)
    return whole.astype(I32).astype(I16), power


def widen(ref, rows):
    return ref[rows, :].astype(I32).astype(F32)


def kernel(
    values, blocks, pairs, inst_out, lag_out,
    plain, index, ring, pair, dense_rows, dense_cols, picked, picks,
    inst, lag, row_sums, col_sums, powers, scales, out1, in1, out2, in2, sums0, sums1, sums2, between,
    ring_send, ring_recv, pair_send, pair_recv, rs_send, rs_recv, sum_send, sum_recv,
):
    x, y, z, core = place()

    def device(dx=0, dy=0, dz=0, dc=0):
        return (
            lax.rem(y + dy + NY, NY) * 2 + lax.rem(core + dc, 2),
            lax.rem(x + dx + NX, NX) * NZ + lax.rem(z + dz + NZ, NZ),
        )

    def send(source, target, send_sem, recv_sem, to):
        copy = pltpu.make_async_remote_copy(
            src_ref=source, dst_ref=target, send_sem=send_sem, recv_sem=recv_sem,
            device_id=to, device_id_type=MESH,
        )
        copy.start()
        return copy

    up, down, other = device(dz=1), device(dz=-1), device(dc=1)
    barrier = pltpu.get_barrier_semaphore()
    partners = [up, down, other]
    partners += [device(dx=d) for d in range(1, NX)] + [device(dy=d) for d in range(1, NY)]
    for to in partners:
        pl.semaphore_signal(barrier, inc=1, device_id=to, device_id_type=MESH)

    prepare(values, blocks, pairs, ring.at[0], plain, index)
    pl.semaphore_wait(barrier, len(partners))

    started = []

    def share(slot, rows, sem):
        started.append(
            send(ring.at[slot, rows], pair.at[slot, rows], pair_send.at[sem], pair_recv.at[sem], other)
        )
        return started[-1]

    whole = pl.ds(0, PACKET)
    low, high = pl.ds(0, HALF), pl.ds(HALF, PACKET - HALF)
    right = send(ring.at[0], ring.at[1], ring_send.at[1], ring_recv.at[1], up)
    left = send(ring.at[0], ring.at[4], ring_send.at[4], ring_recv.at[4], down)
    shared = share(0, whole, 0)

    dense_rows[ROWS:, :] = jnp.ones((16, 4 * B), BF16)
    dense_cols[COLS:, :] = jnp.ones((B, 4 * B), BF16)

    def fill_from(buffer, slot, position):
        lanes = pl.ds(position * B, B)
        fill(buffer.at[slot], lanes, core, z, dense_rows, dense_cols, picked, picks)

    def product(first, depth):
        multiply(first, depth, dense_rows, dense_cols, inst, lag, row_sums, col_sums)

    fill_from(ring, 0, 0)
    shared.wait_recv()
    fill_from(pair, 0, 1)
    product(True, 2 * B)

    for s in range(1, 4):
        right.wait_recv()
        started.append(right)
        if s < 3:
            right = send(ring.at[s], ring.at[s + 1], ring_send.at[s + 1], ring_recv.at[s + 1], up)
        else:
            right = send(ring.at[s, low], ring.at[7, low], ring_send.at[7], ring_recv.at[7], up)
        left.wait_recv()
        started.append(left)
        if s < 3:
            left = send(ring.at[3 + s], ring.at[4 + s], ring_send.at[4 + s], ring_recv.at[4 + s], down)
        else:
            left = send(ring.at[6, high], ring.at[7, high], ring_send.at[8], ring_recv.at[8], down)
        shared = [share(s, whole, s), share(3 + s, whole, 3 + s)]

        def from_ring(n, carry, s=s):
            fill_from(ring, s + 3 * n, n)
            return carry

        lax.fori_loop(0, 2, from_ring, 0)
        for copy in shared:
            copy.wait_recv()

        def from_pair(n, carry, s=s):
            fill_from(pair, s + 3 * n, 2 + n)
            return carry

        lax.fori_loop(0, 2, from_pair, 0)
        product(False, 4 * B)

    right.wait_recv()
    shared = [share(7, low, 7)]
    left.wait_recv()
    shared.append(share(7, high, 8))
    started += [right, left]
    fill_from(ring, 7, 0)
    for copy in shared:
        copy.wait_recv()
    fill_from(pair, 7, 1)
    product(False, 2 * B)

    accs = (inst, lag)
    at = ((x, y), (y, x))
    across = ((device(dx=1), device(dx=-1)), (device(dy=1), device(dy=-1)))
    ways = (across, (across[1], across[0]))

    def message(which, stage, kind, d):
        n = 2 * kind + d
        number = 6 * stage + n
        out, into = ((out1, in1), (out2, in2))[stage]
        copy = send(
            out.at[which, n], into.at[which, n],
            rs_send.at[which, number], rs_recv.at[which, number], ways[which][stage][d],
        )
        started.append(copy)
        return copy

    def scales_of(ref, data, slot):
        power = widen(ref, pl.ds(data, 16))
        scales[slot] = jnp.exp2(power * (1 / STEPS)) * (1 / TOP)

    def decoded(ref, n, slot):
        rows = pl.ds(pl.multiple_of(n * B, B), B)
        return widen(ref, rows) * scales[slot, pl.ds(n, 1), :]

    def write(ref, count, value_of):
        def body(n, carry):
            q, power = encode(value_of(n))
            ref[pl.ds(pl.multiple_of(n * B, B), B), :] = q
            powers[pl.ds(n, 1), :] = power
            return carry

        lax.fori_loop(0, count, body, 0)
        tail = jnp.concatenate([powers[...], jnp.zeros((8, B), F32)], axis=0)
        ref[count * B : count * B + 16, :] = tail.astype(I32).astype(I16)

    powers[...] = jnp.zeros_like(powers)
    col_means = [col_sums[n] * (1 / GROUP) for n in range(2 * NX)]
    for n in range(2 * NX):
        col_sums[n] = col_means[n]

    def centred(which, first, second, i):
        yy, xx = (second, first) if which == 0 else (first, second)
        rows = pl.ds(pl.multiple_of(i * B, B), B)
        mean = col_sums[2 * xx + which, 0:1, :]
        return accs[which][first, second, rows, :] - row_sums[yy, rows, :] * mean

    copies = {}
    for d in range(2):
        for which in range(2):
            first = lax.rem(at[which][0] + 2, 4)
            write(
                out1.at[which, d], 8,
                lambda n, which=which, first=first, d=d: centred(which, first, 2 * d + n // 4, n % 4),
            )
            copies[which, 0, d] = message(which, 0, 0, d)

    diagonal = lax.broadcasted_iota(I32, (B, B), 0) == lax.broadcasted_iota(I32, (B, B), 1)

    def sums_of(yy, carry):
        flat = []
        for i in range(4):
            tile = row_sums[yy, i * B : (i + 1) * B, :]
            flat.append(jnp.sum(jnp.where(diagonal, tile, 0.0), axis=0, keepdims=True))
        for xx in range(NX):
            means = [col_sums[2 * xx + w, 0:1, :] for w in range(2)]
            sums0[xx, yy] = jnp.concatenate(flat + means + means, axis=0)
        return carry

    lax.fori_loop(0, NY, sums_of, 0)
    exchange = []
    for d in range(1, NX):
        exchange.append(
            send(sums0.at[lax.rem(x + d, NX)], sums1.at[x], sum_send.at[d - 1], sum_recv.at[d - 1], device(dx=d))
        )
    sums1[x] = sums0[x]

    for d in range(2):
        for which in range(2):
            first = lax.rem(at[which][0] + 1 + 2 * d, 4)
            write(
                out1.at[which, 2 + d], 8,
                lambda n, which=which, first=first, d=d: centred(which, first, 2 - 2 * d + n // 4, n % 4),
            )
            copies[which, 1, d] = message(which, 0, 1, d)

    for copy in exchange:
        copy.wait_recv()
    started += exchange
    exchange = []
    for d in range(1, NY):
        exchange.append(
            send(
                sums1.at[:, lax.rem(y + d, NY)], sums2.at[pl.ds(pl.multiple_of(NX * y, NX), NX)],
                sum_send.at[2 + d], sum_recv.at[2 + d], device(dy=d),
            )
        )
    sums2[pl.ds(pl.multiple_of(NX * y, NX), NX)] = sums1[:, y]

    for d in range(2):
        for which in range(2):
            copies[which, 0, d].wait_recv()
            first = lax.rem(at[which][0] + 1 + 2 * d, 4)
            scales_of(in1.at[which, d], 8 * B, 0)
            write(
                out1.at[which, 4 + d], 8,
                lambda n, which=which, first=first, d=d: (
                    centred(which, first, 2 * d + n // 4, n % 4) + decoded(in1.at[which, d], n, 0)
                ),
            )
            copies[which, 2, d] = message(which, 0, 2, d)

    for copy in exchange:
        copy.wait_recv()
    started += exchange
    apart = []
    for n in range(6):
        of_groups = sums2[:, n, :]
        apart.append(of_groups - jnp.mean(of_groups, axis=0, keepdims=True))
    for which in range(2):
        for i in range(4):
            between[which, i * B : (i + 1) * B, :] = lax.dot_general(
                apart[i], apart[4 + which], TN,
                precision=lax.Precision.HIGHEST, preferred_element_type=F32,
            )

    for h in range(2):
        for which in range(2):
            a = at[which][0]
            parts = (4, 3) if h == 0 else (2, 5)
            for slot, n in enumerate(parts):
                copies[which, n // 2, n % 2].wait_recv()
                scales_of(in1.at[which, n], 8 * B, slot)

            def total(n, carry, which=which, a=a, h=h, parts=parts):
                second, i = 2 * h + n // 4, n % 4
                value = centred(which, a, second, i)
                for slot, part in enumerate(parts):
                    value = value + decoded(in1.at[which, part], n, slot)
                accs[which][a, second, pl.ds(pl.multiple_of(i * B, B), B), :] = value
                return carry

            lax.fori_loop(0, 8, total, 0)

    def summed(which, second, i):
        return accs[which][at[which][0], second, pl.ds(pl.multiple_of(i * B, B), B), :]

    for d in range(2):
        for which in range(2):
            second = lax.rem(at[which][1] + 2, 4)
            write(
                out2.at[which, d], 2,
                lambda n, which=which, second=second, d=d: summed(which, second, 2 * d + n),
            )
            copies[which, 0, d] = message(which, 1, 0, d)
    for d in range(2):
        for which in range(2):
            second = lax.rem(at[which][1] + 1 + 2 * d, 4)
            write(
                out2.at[which, 2 + d], 2,
                lambda n, which=which, second=second, d=d: summed(which, second, 2 - 2 * d + n),
            )
            copies[which, 1, d] = message(which, 1, 1, d)
    for d in range(2):
        for which in range(2):
            copies[which, 0, d].wait_recv()
            second = lax.rem(at[which][1] + 1 + 2 * d, 4)
            scales_of(in2.at[which, d], 2 * B, 0)
            write(
                out2.at[which, 4 + d], 2,
                lambda n, which=which, second=second, d=d: (
                    summed(which, second, 2 * d + n) + decoded(in2.at[which, d], n, 0)
                ),
            )
            copies[which, 2, d] = message(which, 1, 2, d)
    for h in range(2):
        for which in range(2):
            parts = (4, 3) if h == 0 else (2, 5)
            for slot, n in enumerate(parts):
                copies[which, n // 2, n % 2].wait_recv()
                scales_of(in2.at[which, n], 2 * B, slot)
            for n in range(2):
                rows = slice((2 * h + n) * B, (2 * h + n + 1) * B)
                value = summed(which, at[which][1], 2 * h + n) + between[which, rows, :]
                for slot, part in enumerate(parts):
                    value = value + decoded(in2.at[which, part], n, slot)
                (inst_out, lag_out)[which][rows, :] = value * (1 / PAIRS)
    for copy in started:
        copy.wait_send()


def on_device(frame_values, frame_blocks, lag_pairs):
    chunk = jax.ShapeDtypeStruct((4 * B, B), F32)
    vmem = pl.BlockSpec(memory_space=pltpu.VMEM)
    return pl.pallas_call(
        kernel,
        out_shape=(chunk, chunk),
        in_specs=[vmem] * 3,
        out_specs=(vmem, vmem),
        scratch_shapes=[
            pltpu.VMEM((FRAMES * SLOTS, B), F32),
            pltpu.VMEM((SLOTS, B), F32),
            pltpu.VMEM((NZ, PACKET, B), BF16),
            pltpu.VMEM((NZ, PACKET, B), BF16),
            pltpu.VMEM((ROWS + 16, 4 * B), BF16),
            pltpu.VMEM((COLS + B, 4 * B), BF16),
            pltpu.VMEM((NX * B, 2 * B), BF16),
            pltpu.VMEM((2 * B, B), BF16),
            pltpu.VMEM((NX, NY, 4 * B, B), F32),
            pltpu.VMEM((NY, NX, 4 * B, B), F32),
            pltpu.VMEM((NY, 4 * B, B), F32),
            pltpu.VMEM((2 * NX, 8, B), F32),
            pltpu.VMEM((8, B), F32),
            pltpu.VMEM((2, 16, B), F32),
            pltpu.VMEM((2, 6, FAR, B), I16),
            pltpu.VMEM((2, 6, FAR, B), I16),
            pltpu.VMEM((2, 6, NEAR, B), I16),
            pltpu.VMEM((2, 6, NEAR, B), I16),
            pltpu.VMEM((NX, NY, 8, B), F32),
            pltpu.VMEM((NX, NY, 8, B), F32),
            pltpu.VMEM((NX * NY, 8, B), F32),
            pltpu.VMEM((2, 4 * B, B), F32),
            pltpu.SemaphoreType.DMA((9,)),
            pltpu.SemaphoreType.DMA((9,)),
            pltpu.SemaphoreType.DMA((9,)),
            pltpu.SemaphoreType.DMA((9,)),
            pltpu.SemaphoreType.DMA((2, 12)),
            pltpu.SemaphoreType.DMA((2, 12)),
            pltpu.SemaphoreType.DMA((6,)),
            pltpu.SemaphoreType.DMA((6,)),
        ],
        compiler_params=pltpu.CompilerParams(
            collective_id=0, has_side_effects=True, vmem_limit_bytes=56 << 20
        ),
        name="covariances",
    )(frame_values, frame_blocks.T, lag_pairs.T)


def solution(mesh):
    spec = P(("traj", "feat"))
    return jax.shard_map(
        on_device,
        mesh=mesh,
        in_specs=(spec, spec, spec),
        out_specs=(P("traj", "feat"), P("traj", "feat")),
        check_vma=False,
    )
```

```python
import jax
import jax.numpy as jnp
from jax import lax
from jax.experimental import pallas as pl
from jax.experimental.pallas import tpu as pltpu
from jax.sharding import PartitionSpec as P

MESH = pl.DeviceIdType.MESH
F32, BF16, I16, I32 = jnp.float32, jnp.bfloat16, jnp.int16, jnp.int32
NX, NY, NZ = 4, 4, 8
B = 128
SLOTS = 8
FRAMES = 160
EXTRA = FRAMES - B
IDS = 10 * B
PACKET = IDS + 16
HALF = 5 * B
ROWS = 4 * NY * B
COLS = 2 * NX * B
GROUP = 2 * NZ * B
PAIRS = NX * NY * GROUP
FAR = 4 * B + 16
NEAR = 2 * B + 16
STEPS = 16.0
TOP = 32512.0
NT = (((1,), (1,)), ((), ()))
TN = (((0,), (0,)), ((), ()))


def place():
    t, f = lax.axis_index("traj"), lax.axis_index("feat")
    return f // NZ, t // 2, f % NZ, t % 2


def prepare(values, blocks, pairs, packet, plain, index):
    plain[...] = values[...].astype(F32).reshape(FRAMES * SLOTS, B)
    for k in range(SLOTS):
        tile = plain[pl.ds(k, B, stride=SLOTS), :]
        packet[k * B : (k + 1) * B, :] = tile.T.astype(BF16)
    for g in range(2):
        tile = jnp.concatenate(
            [plain[pl.ds(B * SLOTS + 4 * g + i, EXTRA, stride=SLOTS), :] for i in range(4)], axis=0
        )
        packet[(SLOTS + g) * B : (SLOTS + g + 1) * B, :] = tile.T.astype(BF16)
    rows = [blocks[:, 0:B].astype(F32)]
    index[...] = jnp.zeros_like(index)
    index[:, 0:EXTRA] = blocks[:, B:FRAMES].astype(F32)
    rest = index[...]
    lane = lax.broadcasted_iota(I32, (1, B), 1) // EXTRA
    wide = rest
    for i in range(1, 4):
        wide = wide + pltpu.roll(rest, i * EXTRA, 1)
    for g in range(2):
        row = jnp.zeros((1, B), F32)
        for i in range(4):
            row = jnp.where(lane == i, wide[4 * g + i : 4 * g + i + 1, :], row)
        rows.append(row)
    start = jnp.broadcast_to(pairs[0:1, :], (B, B))
    here = jnp.where(start == lax.broadcasted_iota(I32, (B, B), 0), 1.0, 0.0).astype(BF16)
    lagged = jnp.broadcast_to(pairs[1:2, :], (16, B)).astype(F32).astype(BF16)
    rows.append(lax.dot_general(lagged, here, NT, preferred_element_type=F32)[0:1, :])
    rows.append(jnp.zeros((5, B), F32))
    packet[IDS:PACKET, :] = jnp.concatenate(rows, axis=0).astype(BF16)


def fill(source, lanes, core, z, dense_rows, dense_cols, picked, picks):
    ids = source[IDS:PACKET, :].astype(F32)
    wide = [jnp.broadcast_to(ids[k : k + 1, :], (16, B)).astype(BF16) for k in range(SLOTS + 2)]
    none = jnp.zeros((16, B), BF16)

    def block(number, put):
        want = jnp.full((16, B), number, I32).astype(F32).astype(BF16)
        masks = [w == want for w in wide[:SLOTS]]
        for j in range(0, B, 16):
            got = none
            for k in range(SLOTS):
                got = jnp.where(masks[k], source[k * B + j : k * B + j + 16, :], got)
            put(j, got)
        return want

    lag = jnp.broadcast_to(ids[SLOTS + 2 : SLOTS + 3, :], (B, B))
    down = lax.broadcasted_iota(I32, (B, B), 0)
    picks[0:B, :] = jnp.where(lag == down.astype(F32), 1.0, 0.0).astype(BF16)
    picks[B : 2 * B, :] = jnp.where(lag == (down % EXTRA + B).astype(F32), 1.0, 0.0).astype(BF16)

    def cols_of(n, carry):
        def put(j, got):
            dense_cols[pl.ds(pl.multiple_of(n * 2 * B + j, 16), 16), lanes] = got
            picked[pl.ds(pl.multiple_of(n * B + j, 16), 16), 0:B] = got

        want = block(n * NZ + z, put)
        masks = [wide[SLOTS + g] == want for g in range(2)]
        for j in range(0, B, 16):
            got = none
            for g in range(2):
                tile = source[(SLOTS + g) * B + j : (SLOTS + g) * B + j + 16, :]
                got = jnp.where(masks[g], tile, got)
            picked[pl.ds(pl.multiple_of(n * B + j, 16), 16), B : 2 * B] = got
        return carry

    lax.fori_loop(0, NX, cols_of, 0, unroll=True)
    lags = jnp.dot(picked[...], picks[...], preferred_element_type=F32).astype(BF16)
    for n in range(NX):
        dense_cols[(2 * n + 1) * B : (2 * n + 2) * B, lanes] = lags[n * B : (n + 1) * B, :]

    def rows_of(n, carry):
        def put(j, got):
            dense_rows[pl.ds(pl.multiple_of(n * B + j, 16), 16), lanes] = got

        block(n // 4 * NZ + core * 4 + n % 4, put)
        return carry

    lax.fori_loop(0, 4 * NY, rows_of, 0, unroll=True)


def multiply(q, first, depth, dense_rows, dense_cols, inst, lag, row_sums, col_sums):
    def put(ref, index, value):
        if first:
            ref[index] = value
        else:
            ref[index] += value

    half = ROWS // 2
    height = half + 16 * q
    out = lax.dot_general(
        dense_rows[q * half : q * half + height, 0:depth], dense_cols[:, 0:depth], NT,
        preferred_element_type=F32,
    )
    for h in range(2):
        part = out[h * 4 * B : (h + 1) * 4 * B]
        for x in range(NX):
            put(inst, (x, 2 * q + h), part[:, 2 * x * B : (2 * x + 1) * B])
            put(lag, (2 * q + h, x), part[:, (2 * x + 1) * B : (2 * x + 2) * B])
        put(row_sums, (2 * q + h,), part[:, COLS:])
    if q == 1:
        for n in range(2 * NX):
            put(col_sums, (n,), out[half : half + 8, n * B : (n + 1) * B])


def encode(value):
    top = jnp.max(jnp.abs(value), axis=0, keepdims=True)
    power = jnp.ceil(jnp.log(jnp.maximum(top, 1e-30)) * (STEPS / 0.6931471805599453))
    whole = jnp.floor(value * (jnp.exp2(power * (-1 / STEPS)) * TOP) + 0.5)
    return whole.astype(I32).astype(I16), power


def widen(ref, rows):
    return ref[rows, :].astype(I32).astype(F32)


def kernel(
    values, blocks, pairs, inst_out, lag_out,
    plain, index, ring, pair, dense_rows, dense_cols, picked, picks,
    inst, lag, row_sums, col_sums, powers, scales, out1, in1, out2, in2, sums0, sums1, sums2, between,
    ring_send, ring_recv, pair_send, pair_recv, rs_send, rs_recv, sum_send, sum_recv,
):
    x, y, z, core = place()

    def device(dx=0, dy=0, dz=0, dc=0):
        return (
            lax.rem(y + dy + NY, NY) * 2 + lax.rem(core + dc, 2),
            lax.rem(x + dx + NX, NX) * NZ + lax.rem(z + dz + NZ, NZ),
        )

    def send(source, target, send_sem, recv_sem, to):
        copy = pltpu.make_async_remote_copy(
            src_ref=source, dst_ref=target, send_sem=send_sem, recv_sem=recv_sem,
            device_id=to, device_id_type=MESH,
        )
        copy.start()
        return copy

    up, down, other = device(dz=1), device(dz=-1), device(dc=1)
    barrier = pltpu.get_barrier_semaphore()
    partners = [up, down, other]
    partners += [device(dx=d) for d in range(1, NX)] + [device(dy=d) for d in range(1, NY)]
    for to in partners:
        pl.semaphore_signal(barrier, inc=1, device_id=to, device_id_type=MESH)

    prepare(values, blocks, pairs, ring.at[0], plain, index)
    pl.semaphore_wait(barrier, len(partners))

    started = []
    low, high = pl.ds(0, HALF), pl.ds(HALF, PACKET - HALF)
    pieces = ((low, high), (high, low))
    ways = (up, down)
    coming = {}

    def pass_on(way, s, n):
        rows = pieces[way][n]
        held, there = (3 * way + s if s else 0), (3 * way + s + 1 if s < 3 else 7)
        sem = 2 * there + (way if s == 3 else n)
        coming[way, s + 1, n] = send(
            ring.at[held, rows], ring.at[there, rows], ring_send.at[sem], ring_recv.at[sem], ways[way]
        )
        started.append(coming[way, s + 1, n])

    def arrive(s, n):
        for way in range(2):
            coming[way, s, n].wait_recv()
            if s < 3 or (s == 3 and n == 0):
                pass_on(way, s, n)

    def share(slot, rows, sem):
        started.append(
            send(ring.at[slot, rows], pair.at[slot, rows], pair_send.at[sem], pair_recv.at[sem], other)
        )
        return started[-1]

    whole = pl.ds(0, PACKET)
    for n in range(2):
        for way in range(2):
            pass_on(way, 0, n)
    shared = share(0, whole, 0)

    dense_rows[ROWS:, :] = jnp.ones((16, 4 * B), BF16)
    dense_cols[COLS:, :] = jnp.ones((B, 4 * B), BF16)

    def fill_from(buffer, slot, position):
        lanes = pl.ds(position * B, B)
        fill(buffer.at[slot], lanes, core, z, dense_rows, dense_cols, picked, picks)

    def product(q, first, depth):
        multiply(q, first, depth, dense_rows, dense_cols, inst, lag, row_sums, col_sums)

    fill_from(ring, 0, 0)
    shared.wait_recv()
    fill_from(pair, 0, 1)
    product(0, True, 2 * B)
    product(1, True, 2 * B)
    arrive(1, 0)

    for s in range(1, 4):
        arrive(s, 1)
        shared = [share(s, whole, s), share(3 + s, whole, 3 + s)]

        def from_ring(n, carry, s=s):
            fill_from(ring, s + 3 * n, n)
            return carry

        lax.fori_loop(0, 2, from_ring, 0)
        for copy in shared:
            copy.wait_recv()

        def from_pair(n, carry, s=s):
            fill_from(pair, s + 3 * n, 2 + n)
            return carry

        lax.fori_loop(0, 2, from_pair, 0)
        product(0, False, 4 * B)
        arrive(s + 1, 0)
        if s == 3:
            shared = [share(7, low, 7), share(7, high, 8)]
        product(1, False, 4 * B)

    fill_from(ring, 7, 0)
    for copy in shared:
        copy.wait_recv()
    fill_from(pair, 7, 1)
    product(0, False, 2 * B)
    product(1, False, 2 * B)

    accs = (inst, lag)
    at = ((x, y), (y, x))
    across = ((device(dx=1), device(dx=-1)), (device(dy=1), device(dy=-1)))
    routes = (across, (across[1], across[0]))
    turns = ((2, 1), (3, 0))

    def second_of(which, step):
        return lax.rem(at[which][1] + step, 4)

    def message(which, stage, n):
        number = 12 * stage + n
        d = (n // 2 if stage == 0 else n) % 2
        out, into = ((out1, in1), (out2, in2))[stage]
        copy = send(
            out.at[which, n], into.at[which, n],
            rs_send.at[which, number], rs_recv.at[which, number], routes[which][stage][d],
        )
        started.append(copy)
        copies[which, stage, n] = copy

    def receive(which, stage, n):
        copies[which, stage, n].wait_recv()
        into, data = ((in1, 4 * B), (in2, 2 * B))[stage]
        power = widen(into.at[which, n], pl.ds(data, 16))
        scales[which, 12 * stage + n] = jnp.exp2(power * (1 / STEPS)) * (1 / TOP)

    def decoded(which, stage, n, i):
        into = (in1, in2)[stage]
        rows = pl.ds(pl.multiple_of(i * B, B), B)
        return widen(into.at[which, n], rows) * scales[which, 12 * stage + n, pl.ds(i, 1), :]

    def write(ref, count, value_of):
        def body(n, carry):
            q, power = encode(value_of(n))
            ref[pl.ds(pl.multiple_of(n * B, B), B), :] = q
            powers[pl.ds(n, 1), :] = power
            return carry

        lax.fori_loop(0, count, body, 0, unroll=2)
        tail = jnp.concatenate([powers[...], jnp.zeros((8, B), F32)], axis=0)
        ref[count * B : count * B + 16, :] = tail.astype(I32).astype(I16)

    powers[...] = jnp.zeros_like(powers)
    col_means = [col_sums[n] * (1 / GROUP) for n in range(2 * NX)]
    for n in range(2 * NX):
        col_sums[n] = col_means[n]

    def centred(which, first, second, i):
        yy, xx = (second, first) if which == 0 else (first, second)
        rows = pl.ds(pl.multiple_of(i * B, B), B)
        mean = col_sums[2 * xx + which, 0:1, :]
        return accs[which][first, second, rows, :] - row_sums[yy, rows, :] * mean

    copies = {}
    for m in range(2):
        for d in range(2):
            for which in range(2):
                first, second = lax.rem(at[which][0] + 2, 4), second_of(which, turns[d][m])
                write(
                    out1.at[which, 2 * d + m], 4,
                    lambda i, w=which, f=first, s=second: centred(w, f, s, i),
                )
                message(which, 0, 2 * d + m)

    diagonal = lax.broadcasted_iota(I32, (B, B), 0) == lax.broadcasted_iota(I32, (B, B), 1)

    def sums_of(yy, carry):
        flat = []
        for i in range(4):
            tile = row_sums[yy, i * B : (i + 1) * B, :]
            flat.append(jnp.sum(jnp.where(diagonal, tile, 0.0), axis=0, keepdims=True))
        for xx in range(NX):
            means = [col_sums[2 * xx + w, 0:1, :] for w in range(2)]
            sums0[xx, yy] = jnp.concatenate(flat + means + means, axis=0)
        return carry

    lax.fori_loop(0, NY, sums_of, 0)
    exchange = []
    for d in range(1, NX):
        exchange.append(
            send(sums0.at[lax.rem(x + d, NX)], sums1.at[x], sum_send.at[d - 1], sum_recv.at[d - 1], device(dx=d))
        )
    sums1[x] = sums0[x]

    for m in range(2):
        for d in range(2):
            for which in range(2):
                first, second = lax.rem(at[which][0] + 1 + 2 * d, 4), second_of(which, turns[1 - d][m])
                write(
                    out1.at[which, 4 + 2 * d + m], 4,
                    lambda i, w=which, f=first, s=second: centred(w, f, s, i),
                )
                message(which, 0, 4 + 2 * d + m)

    for copy in exchange:
        copy.wait_recv()
    started += exchange
    exchange = []
    for d in range(1, NY):
        exchange.append(
            send(
                sums1.at[:, lax.rem(y + d, NY)], sums2.at[pl.ds(pl.multiple_of(NX * y, NX), NX)],
                sum_send.at[2 + d], sum_recv.at[2 + d], device(dy=d),
            )
        )
    sums2[pl.ds(pl.multiple_of(NX * y, NX), NX)] = sums1[:, y]

    for m in range(2):
        for d in range(2):
            for which in range(2):
                n = 2 * d + m
                receive(which, 0, n)
                first, second = lax.rem(at[which][0] + 1 + 2 * d, 4), second_of(which, turns[d][m])
                write(
                    out1.at[which, 8 + n], 4,
                    lambda i, w=which, f=first, s=second, n=n: (
                        centred(w, f, s, i) + decoded(w, 0, n, i)
                    ),
                )
                message(which, 0, 8 + n)

    for copy in exchange:
        copy.wait_recv()
    started += exchange
    apart = []
    for n in range(6):
        of_groups = sums2[:, n, :]
        apart.append(of_groups - jnp.mean(of_groups, axis=0, keepdims=True))
    for which in range(2):
        for i in range(4):
            between[which, i * B : (i + 1) * B, :] = lax.dot_general(
                apart[i], apart[4 + which], TN,
                precision=lax.Precision.HIGHEST, preferred_element_type=F32,
            )

    def gathered(which, d, m):
        joint, near = 8 + 2 * d + m, 4 + 2 * (1 - d) + m
        receive(which, 0, joint)
        receive(which, 0, near)
        second = second_of(which, turns[d][m])
        return lambda i: (
            centred(which, at[which][0], second, i) + decoded(which, 0, joint, i) + decoded(which, 0, near, i)
        )

    chunk = {}
    for which in range(2):
        chunk[which, 2] = gathered(which, 0, 0)
        for d in range(2):
            write(out2.at[which, d], 2, lambda n, w=which, d=d: chunk[w, 2](2 * d + n))
            message(which, 1, d)
    for which in range(2):
        chunk[which, 3] = gathered(which, 1, 0)
        write(out2.at[which, 3], 2, lambda n, w=which: chunk[w, 3](n))
        message(which, 1, 3)
    for which in range(2):
        chunk[which, 1] = gathered(which, 0, 1)
        write(out2.at[which, 2], 2, lambda n, w=which: chunk[w, 1](2 + n))
        message(which, 1, 2)
    for d in range(2):
        for which in range(2):
            receive(which, 1, d)
            write(
                out2.at[which, 4 + d], 2,
                lambda n, w=which, d=d: chunk[w, 1 + 2 * d](2 * d + n) + decoded(w, 1, d, n),
            )
            message(which, 1, 4 + d)
    for which in range(2):
        chunk[which, 0] = gathered(which, 1, 1)
    for h in range(2):
        for which in range(2):
            parts = (4, 3) if h == 0 else (2, 5)
            for part in parts:
                receive(which, 1, part)
            for n in range(2):
                i = 2 * h + n
                value = chunk[which, 0](i) + between[which, i * B : (i + 1) * B, :]
                for part in parts:
                    value = value + decoded(which, 1, part, n)
                (inst_out, lag_out)[which][i * B : (i + 1) * B, :] = value * (1 / PAIRS)
    for copy in started:
        copy.wait_send()


def on_device(frame_values, frame_blocks, lag_pairs):
    chunk = jax.ShapeDtypeStruct((4 * B, B), F32)
    vmem = pl.BlockSpec(memory_space=pltpu.VMEM)
    return pl.pallas_call(
        kernel,
        out_shape=(chunk, chunk),
        in_specs=[vmem] * 3,
        out_specs=(vmem, vmem),
        scratch_shapes=[
            pltpu.VMEM((FRAMES * SLOTS, B), F32),
            pltpu.VMEM((SLOTS, B), F32),
            pltpu.VMEM((NZ, PACKET, B), BF16),
            pltpu.VMEM((NZ, PACKET, B), BF16),
            pltpu.VMEM((ROWS + 16, 4 * B), BF16),
            pltpu.VMEM((COLS + B, 4 * B), BF16),
            pltpu.VMEM((NX * B, 2 * B), BF16),
            pltpu.VMEM((2 * B, B), BF16),
            pltpu.VMEM((NX, NY, 4 * B, B), F32),
            pltpu.VMEM((NY, NX, 4 * B, B), F32),
            pltpu.VMEM((NY, 4 * B, B), F32),
            pltpu.VMEM((2 * NX, 8, B), F32),
            pltpu.VMEM((8, B), F32),
            pltpu.VMEM((2, 18, 16, B), F32),
            pltpu.VMEM((2, 12, FAR, B), I16),
            pltpu.VMEM((2, 12, FAR, B), I16),
            pltpu.VMEM((2, 6, NEAR, B), I16),
            pltpu.VMEM((2, 6, NEAR, B), I16),
            pltpu.VMEM((NX, NY, 8, B), F32),
            pltpu.VMEM((NX, NY, 8, B), F32),
            pltpu.VMEM((NX * NY, 8, B), F32),
            pltpu.VMEM((2, 4 * B, B), F32),
            pltpu.SemaphoreType.DMA((2 * NZ,)),
            pltpu.SemaphoreType.DMA((2 * NZ,)),
            pltpu.SemaphoreType.DMA((9,)),
            pltpu.SemaphoreType.DMA((9,)),
            pltpu.SemaphoreType.DMA((2, 18)),
            pltpu.SemaphoreType.DMA((2, 18)),
            pltpu.SemaphoreType.DMA((6,)),
            pltpu.SemaphoreType.DMA((6,)),
        ],
        compiler_params=pltpu.CompilerParams(
            collective_id=0, has_side_effects=True, vmem_limit_bytes=56 << 20
        ),
        name="covariances",
    )(frame_values, frame_blocks.T, lag_pairs.T)


def solution(mesh):
    spec = P(("traj", "feat"))
    return jax.shard_map(
        on_device,
        mesh=mesh,
        in_specs=(spec, spec, spec),
        out_specs=(P("traj", "feat"), P("traj", "feat")),
        check_vma=False,
    )
```

```python
import jax
import jax.numpy as jnp
from jax import lax
from jax.experimental import pallas as pl
from jax.experimental.pallas import tpu as pltpu
from jax.sharding import PartitionSpec as P

MESH = pl.DeviceIdType.MESH
F32, BF16, I16, I32 = jnp.float32, jnp.bfloat16, jnp.int16, jnp.int32
NX, NY, NZ = 4, 4, 8
B = 128
SLOTS = 8
FRAMES = 160
EXTRA = FRAMES - B
IDS = 10 * B
PACKET = IDS + 16
HALF = 5 * B
ROWS = 4 * NY * B
COLS = 2 * NX * B
GROUP = 2 * NZ * B
PAIRS = NX * NY * GROUP
FAR = 4 * B + 16
NEAR = 2 * B + 16
STEPS = 16.0
TOP = 32512.0
NT = (((1,), (1,)), ((), ()))
TN = (((0,), (0,)), ((), ()))


def place():
    t, f = lax.axis_index("traj"), lax.axis_index("feat")
    return f // NZ, t // 2, f % NZ, t % 2


def prepare(values, blocks, pairs, packet, plain, index):
    plain[...] = values[...].astype(F32).reshape(FRAMES * SLOTS, B)
    for k in range(SLOTS):
        tile = plain[pl.ds(k, B, stride=SLOTS), :]
        packet[k * B : (k + 1) * B, :] = tile.T.astype(BF16)
    for g in range(2):
        tile = jnp.concatenate(
            [plain[pl.ds(B * SLOTS + 4 * g + i, EXTRA, stride=SLOTS), :] for i in range(4)], axis=0
        )
        packet[(SLOTS + g) * B : (SLOTS + g + 1) * B, :] = tile.T.astype(BF16)
    rows = [blocks[:, 0:B].astype(F32)]
    index[...] = jnp.zeros_like(index)
    index[:, 0:EXTRA] = blocks[:, B:FRAMES].astype(F32)
    rest = index[...]
    lane = lax.broadcasted_iota(I32, (1, B), 1) // EXTRA
    wide = rest
    for i in range(1, 4):
        wide = wide + pltpu.roll(rest, i * EXTRA, 1)
    for g in range(2):
        row = jnp.zeros((1, B), F32)
        for i in range(4):
            row = jnp.where(lane == i, wide[4 * g + i : 4 * g + i + 1, :], row)
        rows.append(row)
    start = jnp.broadcast_to(pairs[0:1, :], (B, B))
    here = jnp.where(start == lax.broadcasted_iota(I32, (B, B), 0), 1.0, 0.0).astype(BF16)
    lagged = jnp.broadcast_to(pairs[1:2, :], (16, B)).astype(F32).astype(BF16)
    rows.append(lax.dot_general(lagged, here, NT, preferred_element_type=F32)[0:1, :])
    rows.append(jnp.zeros((5, B), F32))
    packet[IDS:PACKET, :] = jnp.concatenate(rows, axis=0).astype(BF16)


def fill(source, lanes, core, z, dense_rows, dense_cols, picked, picks):
    ids = source[IDS:PACKET, :].astype(F32)
    wide = [jnp.broadcast_to(ids[k : k + 1, :], (16, B)).astype(BF16) for k in range(SLOTS + 2)]
    none = jnp.zeros((16, B), BF16)

    def block(number, put):
        want = jnp.full((16, B), number, I32).astype(F32).astype(BF16)
        masks = [w == want for w in wide[:SLOTS]]
        for j in range(0, B, 16):
            got = none
            for k in range(SLOTS):
                got = jnp.where(masks[k], source[k * B + j : k * B + j + 16, :], got)
            put(j, got)
        return want

    lag = jnp.broadcast_to(ids[SLOTS + 2 : SLOTS + 3, :], (B, B))
    down = lax.broadcasted_iota(I32, (B, B), 0)
    picks[0:B, :] = jnp.where(lag == down.astype(F32), 1.0, 0.0).astype(BF16)
    picks[B : 2 * B, :] = jnp.where(lag == (down % EXTRA + B).astype(F32), 1.0, 0.0).astype(BF16)

    def cols_of(n, carry):
        def put(j, got):
            dense_cols[pl.ds(pl.multiple_of(n * 2 * B + j, 16), 16), lanes] = got
            picked[pl.ds(pl.multiple_of(n * B + j, 16), 16), 0:B] = got

        want = block(n * NZ + z, put)
        masks = [wide[SLOTS + g] == want for g in range(2)]
        for j in range(0, B, 16):
            got = none
            for g in range(2):
                tile = source[(SLOTS + g) * B + j : (SLOTS + g) * B + j + 16, :]
                got = jnp.where(masks[g], tile, got)
            picked[pl.ds(pl.multiple_of(n * B + j, 16), 16), B : 2 * B] = got
        return carry

    lax.fori_loop(0, NX, cols_of, 0, unroll=True)
    lags = jnp.dot(picked[...], picks[...], preferred_element_type=F32).astype(BF16)
    for n in range(NX):
        dense_cols[(2 * n + 1) * B : (2 * n + 2) * B, lanes] = lags[n * B : (n + 1) * B, :]

    def rows_of(n, carry):
        def put(j, got):
            dense_rows[pl.ds(pl.multiple_of(n * B + j, 16), 16), lanes] = got

        block(n // 4 * NZ + core * 4 + n % 4, put)
        return carry

    lax.fori_loop(0, 4 * NY, rows_of, 0, unroll=True)


def multiply(q, first, depth, dense_rows, dense_cols, inst, lag, row_sums, col_sums):
    def put(ref, index, value):
        if first:
            ref[index] = value
        else:
            ref[index] += value

    half = ROWS // 2
    height = half + 16 * q
    out = lax.dot_general(
        dense_rows[q * half : q * half + height, 0:depth], dense_cols[:, 0:depth], NT,
        preferred_element_type=F32,
    )
    for h in range(2):
        part = out[h * 4 * B : (h + 1) * 4 * B]
        for x in range(NX):
            put(inst, (x, 2 * q + h), part[:, 2 * x * B : (2 * x + 1) * B])
            put(lag, (2 * q + h, x), part[:, (2 * x + 1) * B : (2 * x + 2) * B])
        put(row_sums, (2 * q + h,), part[:, COLS:])
    if q == 1:
        for n in range(2 * NX):
            put(col_sums, (n,), out[half : half + 8, n * B : (n + 1) * B])


def encode(value):
    top = jnp.max(jnp.abs(value), axis=0, keepdims=True)
    power = jnp.ceil(jnp.log(jnp.maximum(top, 1e-30)) * (STEPS / 0.6931471805599453))
    whole = jnp.floor(value * (jnp.exp2(power * (-1 / STEPS)) * TOP) + 0.5)
    return whole.astype(I32).astype(I16), power


def widen(ref, rows):
    return ref[rows, :].astype(I32).astype(F32)


def kernel(
    values_in, blocks_in, pairs_in, inst_out, lag_out, values, blocks, pairs, load,
    plain, index, ring, pair, dense_rows, dense_cols, picked, picks,
    inst, lag, row_sums, col_sums, powers, scales, out1, in1, out2, in2, sums0, sums1, sums2, between,
    ring_send, ring_recv, pair_send, pair_recv, rs_send, rs_recv, sum_send, sum_recv,
):
    x, y, z, core = place()

    def device(dx=0, dy=0, dz=0, dc=0):
        return (
            lax.rem(y + dy + NY, NY) * 2 + lax.rem(core + dc, 2),
            lax.rem(x + dx + NX, NX) * NZ + lax.rem(z + dz + NZ, NZ),
        )

    def send(source, target, send_sem, recv_sem, to):
        copy = pltpu.make_async_remote_copy(
            src_ref=source, dst_ref=target, send_sem=send_sem, recv_sem=recv_sem,
            device_id=to, device_id_type=MESH,
        )
        copy.start()
        return copy

    up, down, other = device(dz=1), device(dz=-1), device(dc=1)
    loads = []
    for n, (source, target) in enumerate(((values_in, values), (blocks_in, blocks), (pairs_in, pairs))):
        loads.append(pltpu.make_async_copy(source, target, load.at[n]))
        loads[-1].start()
    barrier = pltpu.get_barrier_semaphore()
    partners = [up, down, other]
    partners += [device(dx=d) for d in range(1, NX)] + [device(dy=d) for d in range(1, NY)]
    for to in partners:
        pl.semaphore_signal(barrier, inc=1, device_id=to, device_id_type=MESH)

    for copy in loads:
        copy.wait()
    prepare(values, blocks, pairs, ring.at[0], plain, index)
    pl.semaphore_wait(barrier, len(partners))

    started = []
    low, high = pl.ds(0, HALF), pl.ds(HALF, PACKET - HALF)
    pieces = ((low, high), (high, low))
    ways = (up, down)
    coming = {}

    def pass_on(way, s, n):
        rows = pieces[way][n]
        held, there = (3 * way + s if s else 0), (3 * way + s + 1 if s < 3 else 7)
        sem = 2 * there + (way if s == 3 else n)
        coming[way, s + 1, n] = send(
            ring.at[held, rows], ring.at[there, rows], ring_send.at[sem], ring_recv.at[sem], ways[way]
        )
        started.append(coming[way, s + 1, n])

    def arrive(s, n):
        for way in range(2):
            coming[way, s, n].wait_recv()
            if s < 3 or (s == 3 and n == 0):
                pass_on(way, s, n)

    def share(slot, rows, sem):
        started.append(
            send(ring.at[slot, rows], pair.at[slot, rows], pair_send.at[sem], pair_recv.at[sem], other)
        )
        return started[-1]

    whole = pl.ds(0, PACKET)
    for n in range(2):
        for way in range(2):
            pass_on(way, 0, n)
    shared = share(0, whole, 0)

    dense_rows[ROWS:, :] = jnp.ones((16, 4 * B), BF16)
    dense_cols[COLS:, :] = jnp.ones((B, 4 * B), BF16)

    def fill_from(buffer, slot, position):
        lanes = pl.ds(position * B, B)
        fill(buffer.at[slot], lanes, core, z, dense_rows, dense_cols, picked, picks)

    def product(q, first, depth):
        multiply(q, first, depth, dense_rows, dense_cols, inst, lag, row_sums, col_sums)

    fill_from(ring, 0, 0)
    shared.wait_recv()
    fill_from(pair, 0, 1)
    product(0, True, 2 * B)
    product(1, True, 2 * B)
    arrive(1, 0)

    for s in range(1, 4):
        arrive(s, 1)
        shared = [share(s, whole, s), share(3 + s, whole, 3 + s)]

        def from_ring(n, carry, s=s):
            fill_from(ring, s + 3 * n, n)
            return carry

        lax.fori_loop(0, 2, from_ring, 0)
        for copy in shared:
            copy.wait_recv()

        def from_pair(n, carry, s=s):
            fill_from(pair, s + 3 * n, 2 + n)
            return carry

        lax.fori_loop(0, 2, from_pair, 0)
        product(0, False, 4 * B)
        arrive(s + 1, 0)
        if s == 3:
            shared = [share(7, low, 7), share(7, high, 8)]
        product(1, False, 4 * B)

    fill_from(ring, 7, 0)
    for copy in shared:
        copy.wait_recv()
    fill_from(pair, 7, 1)
    product(0, False, 2 * B)
    product(1, False, 2 * B)

    accs = (inst, lag)
    at = ((x, y), (y, x))
    across = ((device(dx=1), device(dx=-1)), (device(dy=1), device(dy=-1)))
    routes = (across, (across[1], across[0]))
    turns = ((2, 1), (3, 0))

    def second_of(which, step):
        return lax.rem(at[which][1] + step, 4)

    def message(which, stage, n):
        number = 12 * stage + n
        d = (n // 2 if stage == 0 else n) % 2
        out, into = ((out1, in1), (out2, in2))[stage]
        copy = send(
            out.at[which, n], into.at[which, n],
            rs_send.at[which, number], rs_recv.at[which, number], routes[which][stage][d],
        )
        started.append(copy)
        copies[which, stage, n] = copy

    def receive(which, stage, n):
        copies[which, stage, n].wait_recv()
        into, data = ((in1, 4 * B), (in2, 2 * B))[stage]
        power = widen(into.at[which, n], pl.ds(data, 16))
        scales[which, 12 * stage + n] = jnp.exp2(power * (1 / STEPS)) * (1 / TOP)

    def decoded(which, stage, n, i):
        into = (in1, in2)[stage]
        rows = pl.ds(pl.multiple_of(i * B, B), B)
        return widen(into.at[which, n], rows) * scales[which, 12 * stage + n, pl.ds(i, 1), :]

    def write(ref, count, value_of):
        def body(n, carry):
            q, power = encode(value_of(n))
            ref[pl.ds(pl.multiple_of(n * B, B), B), :] = q
            powers[pl.ds(n, 1), :] = power
            return carry

        lax.fori_loop(0, count, body, 0, unroll=2)
        tail = jnp.concatenate([powers[...], jnp.zeros((8, B), F32)], axis=0)
        ref[count * B : count * B + 16, :] = tail.astype(I32).astype(I16)

    powers[...] = jnp.zeros_like(powers)
    col_means = [col_sums[n] * (1 / GROUP) for n in range(2 * NX)]
    for n in range(2 * NX):
        col_sums[n] = col_means[n]

    def centred(which, first, second, i):
        yy, xx = (second, first) if which == 0 else (first, second)
        rows = pl.ds(pl.multiple_of(i * B, B), B)
        mean = col_sums[2 * xx + which, 0:1, :]
        return accs[which][first, second, rows, :] - row_sums[yy, rows, :] * mean

    copies = {}
    for m in range(2):
        for d in range(2):
            for which in range(2):
                first, second = lax.rem(at[which][0] + 2, 4), second_of(which, turns[d][m])
                write(
                    out1.at[which, 2 * d + m], 4,
                    lambda i, w=which, f=first, s=second: centred(w, f, s, i),
                )
                message(which, 0, 2 * d + m)

    diagonal = lax.broadcasted_iota(I32, (B, B), 0) == lax.broadcasted_iota(I32, (B, B), 1)

    def sums_of(yy, carry):
        flat = []
        for i in range(4):
            tile = row_sums[yy, i * B : (i + 1) * B, :]
            flat.append(jnp.sum(jnp.where(diagonal, tile, 0.0), axis=0, keepdims=True))
        for xx in range(NX):
            means = [col_sums[2 * xx + w, 0:1, :] for w in range(2)]
            sums0[xx, yy] = jnp.concatenate(flat + means + means, axis=0)
        return carry

    lax.fori_loop(0, NY, sums_of, 0)
    exchange = []
    for d in range(1, NX):
        exchange.append(
            send(sums0.at[lax.rem(x + d, NX)], sums1.at[x], sum_send.at[d - 1], sum_recv.at[d - 1], device(dx=d))
        )
    sums1[x] = sums0[x]

    for m in range(2):
        for d in range(2):
            for which in range(2):
                first, second = lax.rem(at[which][0] + 1 + 2 * d, 4), second_of(which, turns[1 - d][m])
                write(
                    out1.at[which, 4 + 2 * d + m], 4,
                    lambda i, w=which, f=first, s=second: centred(w, f, s, i),
                )
                message(which, 0, 4 + 2 * d + m)

    for copy in exchange:
        copy.wait_recv()
    started += exchange
    exchange = []
    for d in range(1, NY):
        exchange.append(
            send(
                sums1.at[:, lax.rem(y + d, NY)], sums2.at[pl.ds(pl.multiple_of(NX * y, NX), NX)],
                sum_send.at[2 + d], sum_recv.at[2 + d], device(dy=d),
            )
        )
    sums2[pl.ds(pl.multiple_of(NX * y, NX), NX)] = sums1[:, y]

    for m in range(2):
        for d in range(2):
            for which in range(2):
                n = 2 * d + m
                receive(which, 0, n)
                first, second = lax.rem(at[which][0] + 1 + 2 * d, 4), second_of(which, turns[d][m])
                write(
                    out1.at[which, 8 + n], 4,
                    lambda i, w=which, f=first, s=second, n=n: (
                        centred(w, f, s, i) + decoded(w, 0, n, i)
                    ),
                )
                message(which, 0, 8 + n)

    for copy in exchange:
        copy.wait_recv()
    started += exchange
    apart = []
    for n in range(6):
        of_groups = sums2[:, n, :]
        apart.append(of_groups - jnp.mean(of_groups, axis=0, keepdims=True))
    for which in range(2):
        for i in range(4):
            between[which, i * B : (i + 1) * B, :] = lax.dot_general(
                apart[i], apart[4 + which], TN,
                precision=lax.Precision.HIGHEST, preferred_element_type=F32,
            )

    def gathered(which, d, m):
        joint, near = 8 + 2 * d + m, 4 + 2 * (1 - d) + m
        receive(which, 0, joint)
        receive(which, 0, near)
        second = second_of(which, turns[d][m])
        return lambda i: (
            centred(which, at[which][0], second, i) + decoded(which, 0, joint, i) + decoded(which, 0, near, i)
        )

    chunk = {}
    for which in range(2):
        chunk[which, 2] = gathered(which, 0, 0)
        for d in range(2):
            write(out2.at[which, d], 2, lambda n, w=which, d=d: chunk[w, 2](2 * d + n))
            message(which, 1, d)
    for which in range(2):
        chunk[which, 3] = gathered(which, 1, 0)
        write(out2.at[which, 3], 2, lambda n, w=which: chunk[w, 3](n))
        message(which, 1, 3)
    for which in range(2):
        chunk[which, 1] = gathered(which, 0, 1)
        write(out2.at[which, 2], 2, lambda n, w=which: chunk[w, 1](2 + n))
        message(which, 1, 2)
    for d in range(2):
        for which in range(2):
            receive(which, 1, d)
            write(
                out2.at[which, 4 + d], 2,
                lambda n, w=which, d=d: chunk[w, 1 + 2 * d](2 * d + n) + decoded(w, 1, d, n),
            )
            message(which, 1, 4 + d)
    for which in range(2):
        chunk[which, 0] = gathered(which, 1, 1)
    for h in range(2):
        for which in range(2):
            parts = (4, 3) if h == 0 else (2, 5)
            for part in parts:
                receive(which, 1, part)
            for n in range(2):
                i = 2 * h + n
                value = chunk[which, 0](i) + between[which, i * B : (i + 1) * B, :]
                for part in parts:
                    value = value + decoded(which, 1, part, n)
                (inst_out, lag_out)[which][i * B : (i + 1) * B, :] = value * (1 / PAIRS)
    for copy in started:
        copy.wait_send()


def on_device(frame_values, frame_blocks, lag_pairs):
    chunk = jax.ShapeDtypeStruct((4 * B, B), F32)
    vmem = pl.BlockSpec(memory_space=pltpu.VMEM)
    return pl.pallas_call(
        kernel,
        out_shape=(chunk, chunk),
        in_specs=[pl.BlockSpec(memory_space=pltpu.HBM)] * 3,
        out_specs=(vmem, vmem),
        scratch_shapes=[
            pltpu.VMEM((FRAMES, SLOTS, B), BF16),
            pltpu.VMEM((SLOTS, FRAMES), I32),
            pltpu.VMEM((2, B), I32),
            pltpu.SemaphoreType.DMA((3,)),
            pltpu.VMEM((FRAMES * SLOTS, B), F32),
            pltpu.VMEM((SLOTS, B), F32),
            pltpu.VMEM((NZ, PACKET, B), BF16),
            pltpu.VMEM((NZ, PACKET, B), BF16),
            pltpu.VMEM((ROWS + 16, 4 * B), BF16),
            pltpu.VMEM((COLS + B, 4 * B), BF16),
            pltpu.VMEM((NX * B, 2 * B), BF16),
            pltpu.VMEM((2 * B, B), BF16),
            pltpu.VMEM((NX, NY, 4 * B, B), F32),
            pltpu.VMEM((NY, NX, 4 * B, B), F32),
            pltpu.VMEM((NY, 4 * B, B), F32),
            pltpu.VMEM((2 * NX, 8, B), F32),
            pltpu.VMEM((8, B), F32),
            pltpu.VMEM((2, 18, 16, B), F32),
            pltpu.VMEM((2, 12, FAR, B), I16),
            pltpu.VMEM((2, 12, FAR, B), I16),
            pltpu.VMEM((2, 6, NEAR, B), I16),
            pltpu.VMEM((2, 6, NEAR, B), I16),
            pltpu.VMEM((NX, NY, 8, B), F32),
            pltpu.VMEM((NX, NY, 8, B), F32),
            pltpu.VMEM((NX * NY, 8, B), F32),
            pltpu.VMEM((2, 4 * B, B), F32),
            pltpu.SemaphoreType.DMA((2 * NZ,)),
            pltpu.SemaphoreType.DMA((2 * NZ,)),
            pltpu.SemaphoreType.DMA((9,)),
            pltpu.SemaphoreType.DMA((9,)),
            pltpu.SemaphoreType.DMA((2, 18)),
            pltpu.SemaphoreType.DMA((2, 18)),
            pltpu.SemaphoreType.DMA((6,)),
            pltpu.SemaphoreType.DMA((6,)),
        ],
        compiler_params=pltpu.CompilerParams(
            collective_id=0, has_side_effects=True, vmem_limit_bytes=56 << 20
        ),
        name="covariances",
    )(frame_values, frame_blocks.T, lag_pairs.T)


def solution(mesh):
    spec = P(("traj", "feat"))
    return jax.shard_map(
        on_device,
        mesh=mesh,
        in_specs=(spec, spec, spec),
        out_specs=(P("traj", "feat"), P("traj", "feat")),
        check_vma=False,
    )
```

```python
import jax
import jax.numpy as jnp
from jax import lax
from jax.experimental import pallas as pl
from jax.experimental.pallas import tpu as pltpu
from jax.sharding import PartitionSpec as P

MESH = pl.DeviceIdType.MESH
F32, BF16, I16, I32 = jnp.float32, jnp.bfloat16, jnp.int16, jnp.int32
NX, NY, NZ = 4, 4, 8
B = 128
SLOTS = 8
FRAMES = 160
EXTRA = FRAMES - B
IDS = 10 * B
PACKET = IDS + 16
HALF = 5 * B
ROWS = 4 * NY * B
COLS = 2 * NX * B
GROUP = 2 * NZ * B
PAIRS = NX * NY * GROUP
FAR = 4 * B + 16
NEAR = 2 * B + 16
STEPS = 16.0
TOP = 32512.0
NT = (((1,), (1,)), ((), ()))
TN = (((0,), (0,)), ((), ()))


def place():
    t, f = lax.axis_index("traj"), lax.axis_index("feat")
    return f // NZ, t // 2, f % NZ, t % 2


def prepare(values, blocks, pairs, packet, plain, index):
    plain[...] = values[...].astype(F32).reshape(FRAMES * SLOTS, B)
    for k in range(SLOTS):
        tile = plain[pl.ds(k, B, stride=SLOTS), :]
        packet[k * B : (k + 1) * B, :] = tile.T.astype(BF16)
    for g in range(2):
        tile = jnp.concatenate(
            [plain[pl.ds(B * SLOTS + 4 * g + i, EXTRA, stride=SLOTS), :] for i in range(4)], axis=0
        )
        packet[(SLOTS + g) * B : (SLOTS + g + 1) * B, :] = tile.T.astype(BF16)
    rows = [blocks[:, 0:B].astype(F32)]
    index[...] = jnp.zeros_like(index)
    index[:, 0:EXTRA] = blocks[:, B:FRAMES].astype(F32)
    rest = index[...]
    lane = lax.broadcasted_iota(I32, (1, B), 1) // EXTRA
    wide = rest
    for i in range(1, 4):
        wide = wide + pltpu.roll(rest, i * EXTRA, 1)
    for g in range(2):
        row = jnp.zeros((1, B), F32)
        for i in range(4):
            row = jnp.where(lane == i, wide[4 * g + i : 4 * g + i + 1, :], row)
        rows.append(row)
    start = jnp.broadcast_to(pairs[0:1, :], (B, B))
    here = jnp.where(start == lax.broadcasted_iota(I32, (B, B), 0), 1.0, 0.0).astype(BF16)
    lagged = jnp.broadcast_to(pairs[1:2, :], (16, B)).astype(F32).astype(BF16)
    rows.append(lax.dot_general(lagged, here, NT, preferred_element_type=F32)[0:1, :])
    rows.append(jnp.zeros((5, B), F32))
    packet[IDS:PACKET, :] = jnp.concatenate(rows, axis=0).astype(BF16)


def fill(source, lanes, core, z, dense_rows, dense_cols, picked, picks):
    ids = source[IDS:PACKET, :].astype(F32)
    wide = [jnp.broadcast_to(ids[k : k + 1, :], (16, B)).astype(BF16) for k in range(SLOTS + 2)]
    none = jnp.zeros((16, B), BF16)

    def block(number, put):
        want = jnp.full((16, B), number, I32).astype(F32).astype(BF16)
        masks = [w == want for w in wide[:SLOTS]]
        for j in range(0, B, 16):
            got = none
            for k in range(SLOTS):
                got = jnp.where(masks[k], source[k * B + j : k * B + j + 16, :], got)
            put(j, got)
        return want

    lag = jnp.broadcast_to(ids[SLOTS + 2 : SLOTS + 3, :], (B, B))
    down = lax.broadcasted_iota(I32, (B, B), 0)
    picks[0:B, :] = jnp.where(lag == down.astype(F32), 1.0, 0.0).astype(BF16)
    picks[B : 2 * B, :] = jnp.where(lag == (down % EXTRA + B).astype(F32), 1.0, 0.0).astype(BF16)

    def cols_of(n, carry):
        def put(j, got):
            dense_cols[pl.ds(pl.multiple_of(n * 2 * B + j, 16), 16), lanes] = got
            picked[pl.ds(pl.multiple_of(n * B + j, 16), 16), 0:B] = got

        want = block(n * NZ + z, put)
        masks = [wide[SLOTS + g] == want for g in range(2)]
        for j in range(0, B, 16):
            got = none
            for g in range(2):
                tile = source[(SLOTS + g) * B + j : (SLOTS + g) * B + j + 16, :]
                got = jnp.where(masks[g], tile, got)
            picked[pl.ds(pl.multiple_of(n * B + j, 16), 16), B : 2 * B] = got
        return carry

    lax.fori_loop(0, NX, cols_of, 0, unroll=True)
    lags = jnp.dot(picked[...], picks[...], preferred_element_type=F32).astype(BF16)
    for n in range(NX):
        dense_cols[(2 * n + 1) * B : (2 * n + 2) * B, lanes] = lags[n * B : (n + 1) * B, :]

    def rows_of(n, carry):
        def put(j, got):
            dense_rows[pl.ds(pl.multiple_of(n * B + j, 16), 16), lanes] = got

        block(n // 4 * NZ + core * 4 + n % 4, put)
        return carry

    lax.fori_loop(0, 4 * NY, rows_of, 0, unroll=True)


def multiply(q, first, depth, dense_rows, dense_cols, inst, lag, row_sums, col_sums):
    def put(ref, index, value):
        if first:
            ref[index] = value
        else:
            ref[index] += value

    half = ROWS // 2
    height = half + 16 * q
    out = lax.dot_general(
        dense_rows[q * half : q * half + height, 0:depth], dense_cols[:, 0:depth], NT,
        preferred_element_type=F32,
    )
    for h in range(2):
        part = out[h * 4 * B : (h + 1) * 4 * B]
        for x in range(NX):
            put(inst, (x, 2 * q + h), part[:, 2 * x * B : (2 * x + 1) * B])
            put(lag, (2 * q + h, x), part[:, (2 * x + 1) * B : (2 * x + 2) * B])
        put(row_sums, (2 * q + h,), part[:, COLS:])
    if q == 1:
        for n in range(2 * NX):
            put(col_sums, (n,), out[half : half + 8, n * B : (n + 1) * B])


def encode(value):
    top = jnp.max(jnp.abs(value), axis=0, keepdims=True)
    power = jnp.ceil(jnp.log(jnp.maximum(top, 1e-30)) * (STEPS / 0.6931471805599453))
    whole = jnp.floor(value * (jnp.exp2(power * (-1 / STEPS)) * TOP) + 0.5)
    return whole.astype(I32).astype(I16), power


def widen(ref, rows):
    return ref[rows, :].astype(I32).astype(F32)


def kernel(
    values_in, blocks_in, pairs_in, inst_out, lag_out, values, blocks, pairs, load,
    plain, index, ring, pair, dense_rows, dense_cols, picked, picks,
    inst, lag, row_sums, col_sums, powers, scales, out1, in1, out2, in2, sums0, sums1, sums2, between,
    ring_send, ring_recv, pair_send, pair_recv, rs_send, rs_recv, sum_send, sum_recv,
):
    x, y, z, core = place()

    def device(dx=0, dy=0, dz=0, dc=0):
        return (
            lax.rem(y + dy + NY, NY) * 2 + lax.rem(core + dc, 2),
            lax.rem(x + dx + NX, NX) * NZ + lax.rem(z + dz + NZ, NZ),
        )

    def send(source, target, send_sem, recv_sem, to):
        copy = pltpu.make_async_remote_copy(
            src_ref=source, dst_ref=target, send_sem=send_sem, recv_sem=recv_sem,
            device_id=to, device_id_type=MESH,
        )
        copy.start()
        return copy

    up, down, other = device(dz=1), device(dz=-1), device(dc=1)
    loads = []
    for n, (source, target) in enumerate(((values_in, values), (blocks_in, blocks), (pairs_in, pairs))):
        loads.append(pltpu.make_async_copy(source, target, load.at[n]))
        loads[-1].start()
    barrier = pltpu.get_barrier_semaphore()
    partners = [up, down, other]
    partners += [device(dx=d) for d in range(1, NX)] + [device(dy=d) for d in range(1, NY)]
    for to in partners:
        pl.semaphore_signal(barrier, inc=1, device_id=to, device_id_type=MESH)

    for copy in loads:
        copy.wait()
    prepare(values, blocks, pairs, ring.at[0], plain, index)
    pl.semaphore_wait(barrier, len(partners))

    started = []
    low, high = pl.ds(0, HALF), pl.ds(HALF, PACKET - HALF)
    pieces = ((low, high), (high, low))
    ways = (up, down)
    coming = {}

    def pass_on(way, s, n):
        rows = pieces[way][n]
        held, there = (3 * way + s if s else 0), (3 * way + s + 1 if s < 3 else 7)
        sem = 2 * there + (way if s == 3 else n)
        coming[way, s + 1, n] = send(
            ring.at[held, rows], ring.at[there, rows], ring_send.at[sem], ring_recv.at[sem], ways[way]
        )
        started.append(coming[way, s + 1, n])

    def arrive(s, n):
        for way in range(2):
            coming[way, s, n].wait_recv()
            if s < 3 or (s == 3 and n == 0):
                pass_on(way, s, n)

    def share(slot, rows, sem):
        started.append(
            send(ring.at[slot, rows], pair.at[slot, rows], pair_send.at[sem], pair_recv.at[sem], other)
        )
        return started[-1]

    whole = pl.ds(0, PACKET)
    for n in range(2):
        for way in range(2):
            pass_on(way, 0, n)
    shared = share(0, whole, 0)

    dense_rows[ROWS:, :] = jnp.ones((16, 4 * B), BF16)
    dense_cols[COLS:, :] = jnp.ones((B, 4 * B), BF16)

    def fill_from(buffer, slot, position):
        lanes = pl.ds(position * B, B)
        fill(buffer.at[slot], lanes, core, z, dense_rows, dense_cols, picked, picks)

    def product(q, first, depth):
        multiply(q, first, depth, dense_rows, dense_cols, inst, lag, row_sums, col_sums)

    fill_from(ring, 0, 0)
    shared.wait_recv()
    fill_from(pair, 0, 1)
    product(0, True, 2 * B)
    product(1, True, 2 * B)
    arrive(1, 0)

    for s in range(1, 4):
        arrive(s, 1)
        shared = [share(s, whole, s), share(3 + s, whole, 3 + s)]

        def from_ring(n, carry, s=s):
            fill_from(ring, s + 3 * n, n)
            return carry

        lax.fori_loop(0, 2, from_ring, 0)
        for copy in shared:
            copy.wait_recv()

        def from_pair(n, carry, s=s):
            fill_from(pair, s + 3 * n, 2 + n)
            return carry

        lax.fori_loop(0, 2, from_pair, 0)
        product(0, False, 4 * B)
        arrive(s + 1, 0)
        if s == 3:
            shared = [share(7, low, 7), share(7, high, 8)]
        product(1, False, 4 * B)

    fill_from(ring, 7, 0)
    for copy in shared:
        copy.wait_recv()
    fill_from(pair, 7, 1)
    product(0, False, 2 * B)
    product(1, False, 2 * B)

    accs = (inst, lag)
    at = ((x, y), (y, x))
    across = ((device(dx=1), device(dx=-1)), (device(dy=1), device(dy=-1)))
    routes = (across, (across[1], across[0]))
    turns = ((2, 1), (3, 0))

    def second_of(which, step):
        return lax.rem(at[which][1] + step, 4)

    def message(which, stage, n):
        number = 12 * stage + n
        d = (n // 2 if stage == 0 else n) % 2
        out, into = ((out1, in1), (out2, in2))[stage]
        copy = send(
            out.at[which, n], into.at[which, n],
            rs_send.at[which, number], rs_recv.at[which, number], routes[which][stage][d],
        )
        started.append(copy)
        copies[which, stage, n] = copy

    def receive(which, stage, n):
        copies[which, stage, n].wait_recv()
        into, data = ((in1, 4 * B), (in2, 2 * B))[stage]
        power = widen(into.at[which, n], pl.ds(data, 16))
        scales[which, 12 * stage + n] = jnp.exp2(power * (1 / STEPS)) * (1 / TOP)

    def decoded(which, stage, n, i):
        into = (in1, in2)[stage]
        rows = pl.ds(pl.multiple_of(i * B, B), B)
        return widen(into.at[which, n], rows) * scales[which, 12 * stage + n, pl.ds(i, 1), :]

    def write(ref, count, value_of):
        def body(n, carry):
            q, power = encode(value_of(n))
            ref[pl.ds(pl.multiple_of(n * B, B), B), :] = q
            powers[pl.ds(n, 1), :] = power
            return carry

        lax.fori_loop(0, count, body, 0, unroll=True)
        tail = jnp.concatenate([powers[...], jnp.zeros((8, B), F32)], axis=0)
        ref[count * B : count * B + 16, :] = tail.astype(I32).astype(I16)

    powers[...] = jnp.zeros_like(powers)
    col_means = [col_sums[n] * (1 / GROUP) for n in range(2 * NX)]
    for n in range(2 * NX):
        col_sums[n] = col_means[n]

    def centred(which, first, second, i):
        yy, xx = (second, first) if which == 0 else (first, second)
        rows = pl.ds(pl.multiple_of(i * B, B), B)
        mean = col_sums[2 * xx + which, 0:1, :]
        return accs[which][first, second, rows, :] - row_sums[yy, rows, :] * mean

    copies = {}
    for m in range(2):
        for d in range(2):
            for which in range(2):
                first, second = lax.rem(at[which][0] + 2, 4), second_of(which, turns[d][m])
                write(
                    out1.at[which, 2 * d + m], 4,
                    lambda i, w=which, f=first, s=second: centred(w, f, s, i),
                )
                message(which, 0, 2 * d + m)

    diagonal = lax.broadcasted_iota(I32, (B, B), 0) == lax.broadcasted_iota(I32, (B, B), 1)

    def sums_of(yy, carry):
        flat = []
        for i in range(4):
            tile = row_sums[yy, i * B : (i + 1) * B, :]
            flat.append(jnp.sum(jnp.where(diagonal, tile, 0.0), axis=0, keepdims=True))
        for xx in range(NX):
            means = [col_sums[2 * xx + w, 0:1, :] for w in range(2)]
            sums0[xx, yy] = jnp.concatenate(flat + means + means, axis=0)
        return carry

    lax.fori_loop(0, NY, sums_of, 0)
    exchange = []
    for d in range(1, NX):
        exchange.append(
            send(sums0.at[lax.rem(x + d, NX)], sums1.at[x], sum_send.at[d - 1], sum_recv.at[d - 1], device(dx=d))
        )
    sums1[x] = sums0[x]

    for m in range(2):
        for d in range(2):
            for which in range(2):
                first, second = lax.rem(at[which][0] + 1 + 2 * d, 4), second_of(which, turns[1 - d][m])
                write(
                    out1.at[which, 4 + 2 * d + m], 4,
                    lambda i, w=which, f=first, s=second: centred(w, f, s, i),
                )
                message(which, 0, 4 + 2 * d + m)

    for copy in exchange:
        copy.wait_recv()
    started += exchange
    exchange = []
    for d in range(1, NY):
        exchange.append(
            send(
                sums1.at[:, lax.rem(y + d, NY)], sums2.at[pl.ds(pl.multiple_of(NX * y, NX), NX)],
                sum_send.at[2 + d], sum_recv.at[2 + d], device(dy=d),
            )
        )
    sums2[pl.ds(pl.multiple_of(NX * y, NX), NX)] = sums1[:, y]

    for m in range(2):
        for d in range(2):
            for which in range(2):
                n = 2 * d + m
                receive(which, 0, n)
                first, second = lax.rem(at[which][0] + 1 + 2 * d, 4), second_of(which, turns[d][m])
                write(
                    out1.at[which, 8 + n], 4,
                    lambda i, w=which, f=first, s=second, n=n: (
                        centred(w, f, s, i) + decoded(w, 0, n, i)
                    ),
                )
                message(which, 0, 8 + n)

    for copy in exchange:
        copy.wait_recv()
    started += exchange
    apart = []
    for n in range(6):
        of_groups = sums2[:, n, :]
        apart.append(of_groups - jnp.mean(of_groups, axis=0, keepdims=True))
    for which in range(2):
        for i in range(4):
            between[which, i * B : (i + 1) * B, :] = lax.dot_general(
                apart[i], apart[4 + which], TN,
                precision=lax.Precision.HIGHEST, preferred_element_type=F32,
            )

    def gathered(which, d, m):
        joint, near = 8 + 2 * d + m, 4 + 2 * (1 - d) + m
        receive(which, 0, joint)
        receive(which, 0, near)
        second = second_of(which, turns[d][m])
        return lambda i: (
            centred(which, at[which][0], second, i) + decoded(which, 0, joint, i) + decoded(which, 0, near, i)
        )

    chunk = {}
    for which in range(2):
        chunk[which, 2] = gathered(which, 0, 0)
        for d in range(2):
            write(out2.at[which, d], 2, lambda n, w=which, d=d: chunk[w, 2](2 * d + n))
            message(which, 1, d)
    for which in range(2):
        chunk[which, 3] = gathered(which, 1, 0)
        write(out2.at[which, 3], 2, lambda n, w=which: chunk[w, 3](n))
        message(which, 1, 3)
    for which in range(2):
        chunk[which, 1] = gathered(which, 0, 1)
        write(out2.at[which, 2], 2, lambda n, w=which: chunk[w, 1](2 + n))
        message(which, 1, 2)
    for d in range(2):
        for which in range(2):
            receive(which, 1, d)
            write(
                out2.at[which, 4 + d], 2,
                lambda n, w=which, d=d: chunk[w, 1 + 2 * d](2 * d + n) + decoded(w, 1, d, n),
            )
            message(which, 1, 4 + d)
    for which in range(2):
        chunk[which, 0] = gathered(which, 1, 1)
    for h in range(2):
        for which in range(2):
            parts = (4, 3) if h == 0 else (2, 5)
            for part in parts:
                receive(which, 1, part)
            for n in range(2):
                i = 2 * h + n
                value = chunk[which, 0](i) + between[which, i * B : (i + 1) * B, :]
                for part in parts:
                    value = value + decoded(which, 1, part, n)
                (inst_out, lag_out)[which][i * B : (i + 1) * B, :] = value * (1 / PAIRS)
    for copy in started:
        copy.wait_send()


def on_device(frame_values, frame_blocks, lag_pairs):
    chunk = jax.ShapeDtypeStruct((4 * B, B), F32)
    vmem = pl.BlockSpec(memory_space=pltpu.VMEM)
    return pl.pallas_call(
        kernel,
        out_shape=(chunk, chunk),
        in_specs=[pl.BlockSpec(memory_space=pltpu.HBM)] * 3,
        out_specs=(vmem, vmem),
        scratch_shapes=[
            pltpu.VMEM((FRAMES, SLOTS, B), BF16),
            pltpu.VMEM((SLOTS, FRAMES), I32),
            pltpu.VMEM((2, B), I32),
            pltpu.SemaphoreType.DMA((3,)),
            pltpu.VMEM((FRAMES * SLOTS, B), F32),
            pltpu.VMEM((SLOTS, B), F32),
            pltpu.VMEM((NZ, PACKET, B), BF16),
            pltpu.VMEM((NZ, PACKET, B), BF16),
            pltpu.VMEM((ROWS + 16, 4 * B), BF16),
            pltpu.VMEM((COLS + B, 4 * B), BF16),
            pltpu.VMEM((NX * B, 2 * B), BF16),
            pltpu.VMEM((2 * B, B), BF16),
            pltpu.VMEM((NX, NY, 4 * B, B), F32),
            pltpu.VMEM((NY, NX, 4 * B, B), F32),
            pltpu.VMEM((NY, 4 * B, B), F32),
            pltpu.VMEM((2 * NX, 8, B), F32),
            pltpu.VMEM((8, B), F32),
            pltpu.VMEM((2, 18, 16, B), F32),
            pltpu.VMEM((2, 12, FAR, B), I16),
            pltpu.VMEM((2, 12, FAR, B), I16),
            pltpu.VMEM((2, 6, NEAR, B), I16),
            pltpu.VMEM((2, 6, NEAR, B), I16),
            pltpu.VMEM((NX, NY, 8, B), F32),
            pltpu.VMEM((NX, NY, 8, B), F32),
            pltpu.VMEM((NX * NY, 8, B), F32),
            pltpu.VMEM((2, 4 * B, B), F32),
            pltpu.SemaphoreType.DMA((2 * NZ,)),
            pltpu.SemaphoreType.DMA((2 * NZ,)),
            pltpu.SemaphoreType.DMA((9,)),
            pltpu.SemaphoreType.DMA((9,)),
            pltpu.SemaphoreType.DMA((2, 18)),
            pltpu.SemaphoreType.DMA((2, 18)),
            pltpu.SemaphoreType.DMA((6,)),
            pltpu.SemaphoreType.DMA((6,)),
        ],
        compiler_params=pltpu.CompilerParams(
            collective_id=0, has_side_effects=True, vmem_limit_bytes=56 << 20
        ),
        name="covariances",
    )(frame_values, frame_blocks.T, lag_pairs.T)


def solution(mesh):
    spec = P(("traj", "feat"))
    return jax.shard_map(
        on_device,
        mesh=mesh,
        in_specs=(spec, spec, spec),
        out_specs=(P("traj", "feat"), P("traj", "feat")),
        check_vma=False,
    )
```
